32 devices in a mesh: layer: 2 (over core), row: 4 (over y, x), col: 4 (over z).
Axes of the slice: x: 2, y: 2, z: 4, core: 2. Of those that a mesh axis runs over, the one named last changes fastest.
Arguments:
- rhs_sub: float32 [2, 3, 1, 4, 256, 512], P('layer', None, None, 'row', 'col'), may hold values from -6 to 6
- rhs_top: float32 [1, 4, 256, 512], P(None, 'row', 'col'), may hold values from -6 to 6
- lower_inv_sub: float32 [2, 3, 1, 4, 256, 256], P('layer', None, None, 'row', 'col'), as said below
- lower_inv_top: float32 [1, 4, 256, 256], P(None, 'row', 'col'), as said below
- upper_inv_sub: float32 [2, 3, 1, 4, 256, 256], P('layer', None, None, 'row', 'col'), as said below
- upper_inv_top: float32 [1, 4, 256, 256], P(None, 'row', 'col'), as said below
- lower_sub: float32 [2, 3, 1, 4, 1, 4, 256, 256], P('layer', None, None, 'row', None, 'col'), may hold values from -0.1875 to 0.1875
- lower_top: float32 [2, 3, 1, 4, 1, 4, 256, 256], P('layer', None, None, 'row', None, 'col'), may hold values from -0.109375 to 0.109375
- upper_sub: float32 [2, 3, 1, 4, 1, 4, 256, 256], P('layer', None, None, 'row', None, 'col'), may hold values from -0.125 to 0.125
- upper_top: float32 [2, 3, 1, 4, 1, 4, 256, 256], P('layer', None, None, 'row', None, 'col'), may hold values from -0.1875 to 0.1875
- block_pattern: int32 [2, 4, 3, 1, 4, 1, 4], P('layer', None, None, None, 'row', None, 'col'), may hold values 0 or 1
Outputs:
- solution_sub: float32 [2, 3, 1, 4, 256, 512], P('layer', None, None, 'row', 'col')
- solution_top: float32 [1, 4, 256, 512], P(None, 'row', 'col')
The draws below stay inside these ranges and needn't reach their ends.
Inputs may be any that keep to these rules, and one draw needn't show every extreme that they name: `lower_inv_sub`: every 256 x 256 block is lower triangular with unit diagonal. `lower_inv_top`: every 256 x 256 block is lower triangular with unit diagonal. `upper_inv_sub`: every 256 x 256 block is upper triangular with unit diagonal. `upper_inv_top`: every 256 x 256 block is upper triangular with unit diagonal.
All inputs are finite; a program needn't handle non-finite values. No bound on the sum of `block_pattern` on one device may be relied on, other than what follows from the above.
Results may differ from the reference program's by a relative error of at most 0.00014.
Values sent between devices are 32-bit elements; how exact they have to be, the bound alone decides.
A program may use at most 64 MiB of HBM per device.

```python
import math
import jax
import jax.numpy as jnp
from jax import lax

W = 256
NRHS = 512
SN_ROW = 1
LAYERS = 2
GRID = 4


def unit_triangle(noise, lower):
    shape = noise.shape
    down_index = lax.broadcasted_iota(jnp.int32, shape, len(shape) - 2)
    across_index = lax.broadcasted_iota(jnp.int32, shape, len(shape) - 1)
    strict = down_index > across_index if lower else down_index < across_index
    scaled = noise * (0.8 / math.sqrt(W))
    return jnp.where(down_index == across_index, 1.0, jnp.where(strict, scaled, 0.0)).astype(jnp.float32)


def draw_noise(key, shape):
    return jax.random.normal(key, shape, jnp.float32)


def draw_lower_inv_sub(key, part):
    return unit_triangle(draw_noise(key, (LAYERS, 3, SN_ROW, GRID, W, W)), True)


def draw_lower_inv_top(key, part):
    return unit_triangle(draw_noise(key, (SN_ROW, GRID, W, W)), True)


def draw_upper_inv_sub(key, part):
    return unit_triangle(draw_noise(key, (LAYERS, 3, SN_ROW, GRID, W, W)), False)


def draw_upper_inv_top(key, part):
    return unit_triangle(draw_noise(key, (SN_ROW, GRID, W, W)), False)


def plant(drawn, key, least, top_value):
    index_at = [jax.random.randint(jax.random.fold_in(key, axis), (), 0, length) for axis, length in enumerate(drawn.shape)]
    main_axis = drawn.shape.index(max(drawn.shape))
    beside = index_at[:main_axis] + [(index_at[main_axis] + 1) % drawn.shape[main_axis]] + index_at[main_axis + 1:]
    return drawn.at[tuple(index_at)].set(least).at[tuple(beside)].set(top_value)


def spiked(result, own_key, source, target, shards_of, factor):
    def block_of(axis_at):
        return (jnp.arange(result.shape[axis_at]) // (result.shape[axis_at] // shards_of)).reshape((-1,) + (1,) * (result.ndim - 1 - axis_at))

    first = jax.random.permutation(own_key, shards_of)[block_of(target)]
    second = (block_of(target) + shards_of // 2) % shards_of
    return jnp.where((block_of(source) == first) | (block_of(source) == second), factor * result, result)


def level_of(stream_key, dims, shards, least, top_value):
    def one(position, blocks):
        heights = jax.random.uniform(jax.random.fold_in(jax.random.fold_in(stream_key, 6), position), (blocks,), jnp.float32, least / len(shards), top_value / len(shards))
        return jnp.repeat(jnp.exp(heights), dims[position] // blocks).reshape((-1,) + (1,) * (len(dims) - position - 1))

    gain = one(*shards[0])
    for cut in shards[1:]:
        gain = gain * one(*cut)
    return gain


def scatter_about(own_key, dims, deviation, bound, pieces=(), held_as=jnp.bfloat16):
    entries = deviation * jax.random.normal(own_key, dims, jnp.float32)
    if pieces:
        entries = entries * level_of(own_key, dims, pieces, -0.22, 0.18)
    return jnp.clip(entries, -bound, bound).astype(held_as)


def heavy_noise(own_key, extent, width, most, split, heavy, dtype=jnp.bfloat16):
    drawn = width * jax.random.normal(own_key, extent, jnp.float32)
    if split:
        drawn = drawn * level_of(own_key, extent, split, -0.22, 0.18)
    return jnp.clip(spiked(drawn, jax.random.fold_in(own_key, 3), *heavy), -most, most).astype(dtype)


def setup_inputs(seed: int = 0) -> dict:
    key_list = jax.random.split(jax.random.key(seed), 12)
    return {
        "rhs_sub": scatter_about(key_list[0], (LAYERS, 3, SN_ROW, GRID, W, NRHS), 1.0, 6.0, ((0, 2), (3, 4), (4, 4)), jnp.float32),
        "rhs_top": scatter_about(key_list[1], (SN_ROW, GRID, W, NRHS), 1.0, 6.0, ((1, 4), (2, 4)), jnp.float32),
        "lower_inv_sub": draw_lower_inv_sub(jax.random.fold_in(key_list[11], 71), 0),
        "lower_inv_top": draw_lower_inv_top(jax.random.fold_in(key_list[11], 71), 0),
        "upper_inv_sub": draw_upper_inv_sub(jax.random.fold_in(key_list[11], 71), 0),
        "upper_inv_top": draw_upper_inv_top(jax.random.fold_in(key_list[11], 71), 0),
        "lower_sub": heavy_noise(key_list[6], (LAYERS, 3, SN_ROW, GRID, SN_ROW, GRID, W, W), (2 * W * SN_ROW * GRID) ** -0.5, 0.1875, ((0, 2), (3, 4), (5, 4)), (5, 6, 4, 2.0), jnp.float32),
        "lower_top": heavy_noise(key_list[7], (LAYERS, 3, SN_ROW, GRID, SN_ROW, GRID, W, W), (3 * LAYERS * W * SN_ROW * GRID) ** -0.5, 0.109375, ((0, 2), (3, 4), (5, 4)), (5, 6, 4, 2.0), jnp.float32),
        "upper_sub": heavy_noise(key_list[8], (LAYERS, 3, SN_ROW, GRID, SN_ROW, GRID, W, W), (4 * W * SN_ROW * GRID) ** -0.5, 0.125, ((0, 2), (3, 4), (5, 4)), (5, 6, 4, 2.0), jnp.float32),
        "upper_top": heavy_noise(key_list[9], (LAYERS, 3, SN_ROW, GRID, SN_ROW, GRID, W, W), (2 * W * SN_ROW * GRID) ** -0.5, 0.1875, ((0, 2), (3, 4), (5, 4)), (5, 6, 4, 2.0), jnp.float32),
        "block_pattern": plant((jax.random.randint(key_list[10], (LAYERS, 4, 3, SN_ROW, GRID, SN_ROW, GRID), 0, 4) < 3).astype(jnp.int32), jax.random.fold_in(key_list[10], 1), 0, 1),
    }


HIGHEST = lax.Precision.HIGHEST


def apply_inverse(inverse, block):
    return jnp.einsum('...ab,...bn->...an', inverse, block, precision=HIGHEST)


def couple(blocks, pattern, solution):
    masked = blocks * pattern[..., None, None].astype(jnp.float32)
    return jnp.einsum('tgsqab,sqbn->tgan', masked, solution, precision=HIGHEST)


def reference(rhs_sub, rhs_top, lower_inv_sub, lower_inv_top, upper_inv_sub, upper_inv_top, lower_sub, lower_top, upper_sub, upper_top, block_pattern):
    forward = []
    top_sum = jnp.zeros(rhs_top.shape, jnp.float32)
    for layer_index in range(LAYERS):
        pattern_layer = block_pattern[layer_index]
        fore_zero = apply_inverse(lower_inv_sub[layer_index, 0], rhs_sub[layer_index, 0])
        fore_one = apply_inverse(lower_inv_sub[layer_index, 1], rhs_sub[layer_index, 1] - couple(lower_sub[layer_index, 0], pattern_layer[0, 0], fore_zero))
        fore_two = apply_inverse(lower_inv_sub[layer_index, 2], rhs_sub[layer_index, 2] - couple(lower_sub[layer_index, 1], pattern_layer[0, 1], fore_zero) - couple(lower_sub[layer_index, 2], pattern_layer[0, 2], fore_one))
        top_sum = top_sum + couple(lower_top[layer_index, 0], pattern_layer[1, 0], fore_zero)
        top_sum = top_sum + couple(lower_top[layer_index, 1], pattern_layer[1, 1], fore_one)
        top_sum = top_sum + couple(lower_top[layer_index, 2], pattern_layer[1, 2], fore_two)
        forward.append((fore_zero, fore_one, fore_two))
    fore_top = apply_inverse(lower_inv_top, rhs_top - top_sum)
    final_top = apply_inverse(upper_inv_top, fore_top)
    finals = []
    for layer_index in range(LAYERS):
        pattern_layer = block_pattern[layer_index]
        fore_zero, fore_one, fore_two = forward[layer_index]
        final_two = apply_inverse(upper_inv_sub[layer_index, 2], fore_two - couple(upper_top[layer_index, 2], pattern_layer[3, 2], final_top))
        final_one = apply_inverse(upper_inv_sub[layer_index, 1], fore_one - couple(upper_sub[layer_index, 2], pattern_layer[2, 2], final_two) - couple(upper_top[layer_index, 1], pattern_layer[3, 1], final_top))
        final_zero = apply_inverse(upper_inv_sub[layer_index, 0], fore_zero - couple(upper_sub[layer_index, 0], pattern_layer[2, 0], final_one) - couple(upper_sub[layer_index, 1], pattern_layer[2, 1], final_two) - couple(upper_top[layer_index, 0], pattern_layer[3, 0], final_top))
        finals.append(jnp.stack([final_zero, final_one, final_two]))
    solution_sub = jnp.stack(finals)
    return solution_sub, final_top
```

```python
import functools
import jax
import jax.numpy as jnp
from jax import lax
from jax.experimental import pallas as pl
from jax.experimental.pallas import tpu as pltpu
from jax.sharding import PartitionSpec as P

HIGHEST = lax.Precision.HIGHEST
MESH = pl.DeviceIdType.MESH
LEVELS = 3


def dot(a, b):
    return jnp.dot(a, b, precision=HIGHEST, preferred_element_type=jnp.float32)


def kernel(
    layers,
    grid,
    pattern,
    rhs_sub,
    rhs_top,
    lower_inv_sub,
    lower_inv_top,
    upper_inv_sub,
    upper_inv_top,
    lower_sub,
    lower_top,
    upper_sub,
    upper_top,
    out_sub,
    out_top,
    coupling,
    rhs_split,
    rhs_stage,
    rhs_full,
    inv_stage,
    inv_full,
    part,
    arrived,
    solved,
    cross,
    out_stage,
    out_full,
    coupling_sem,
    rhs_sem,
    rhs_z_sem,
    inv_sem,
    inv_z_sem,
    part_sem,
    cross_sem,
    out_z_sem,
    out_sem,
):
    layer, row, col = lax.axis_index("layer"), lax.axis_index("row"), lax.axis_index("col")
    width = part.shape[2]
    columns = part.shape[3]
    others = range(1, grid)

    def ahead(me, step, count=grid):
        return lax.rem(me + step, count)

    barrier = pltpu.get_barrier_semaphore()
    for step in others:
        pl.semaphore_signal(barrier, inc=1, device_id=(layer, ahead(row, step), col), device_id_type=MESH)
        pl.semaphore_signal(barrier, inc=1, device_id=(layer, row, ahead(col, step)), device_id_type=MESH)
    for step in range(1, layers):
        pl.semaphore_signal(
            barrier, inc=1, device_id=(ahead(layer, step, layers), row, col), device_id_type=MESH
        )

    def remote(source, target, sems, index, step, device):
        return pltpu.make_async_remote_copy(
            src_ref=source,
            dst_ref=target,
            send_sem=sems.at[0, index, step - 1],
            recv_sem=sems.at[1, index, step - 1],
            device_id=device,
            device_id_type=MESH,
        )

    sources = (
        (lower_sub, 0, 0),
        (lower_sub, 1, 0),
        (lower_sub, 2, 0),
        (lower_top, 0, 1),
        (lower_top, 1, 1),
        (lower_top, 2, 1),
        (upper_top, 2, 3),
        (upper_top, 1, 3),
        (upper_sub, 2, 2),
        (upper_top, 0, 3),
        (upper_sub, 1, 2),
        (upper_sub, 0, 2),
    )
    inverses = tuple(lower_inv_sub.at[k] for k in range(LEVELS)) + (lower_inv_top,)
    inverses += tuple(upper_inv_sub.at[k] for k in range(LEVELS)) + (upper_inv_top,)
    rights = tuple(rhs_sub.at[k] for k in range(LEVELS)) + (rhs_top,)

    def mask(k):
        ref, pair, kind = sources[k]
        coupling[k, row] = ref[pair] * pattern[kind * LEVELS + pair].astype(jnp.float32)

    def coupling_copy(k, step):
        return remote(
            coupling.at[k, row], coupling.at[k, row], coupling_sem, k, step, (layer, ahead(row, step), col)
        )

    def rhs_copy(k, step):
        to = ahead(row, step)
        return remote(rhs_split.at[k, to], rhs_stage.at[k, row], rhs_sem, k, step, (layer, to, col))

    def inv_copy(k, step):
        return remote(inverses[k], inv_stage.at[k, row], inv_sem, k, step, (layer, ahead(row, step), col))

    def rhs_z_copy(k, step):
        to = ahead(col, step)
        return remote(rhs_stage.at[k, to], rhs_full.at[k, col], rhs_z_sem, k, step, (layer, row, to))

    def inv_z_copy(k, step):
        to = ahead(col, step)
        return remote(inv_stage.at[k, to], inv_full.at[k, col], inv_z_sem, k, step, (layer, row, to))

    def part_copy(k, step):
        to = ahead(col, step)
        return remote(part.at[k, to], arrived.at[k, col], part_sem, k, step, (layer, row, to))

    def cross_copy(step):
        return remote(
            cross.at[0], cross.at[step], cross_sem, 0, step, (ahead(layer, step, layers), row, col)
        )

    rows = width // grid

    def out_z_copy(k, step):
        to = ahead(col, step)
        return remote(solved.at[k, to], out_stage.at[k, col], out_z_sem, k, step, (layer, row, to))

    def out_copy(k, step):
        to = ahead(row, step)
        return remote(out_stage.at[k, to], out_full.at[k, row], out_sem, k, step, (layer, to, col))

    sent = []

    def start(make, k):
        for step in others:
            copy = make(k, step)
            copy.start()
            sent.append(copy)

    def arrive(make, k):
        for step in others:
            make(k, step).wait_recv()

    def spread_coupling(k):
        mask(k)
        start(coupling_copy, k)

    def rhs_row(k):
        start(rhs_copy, k)
        rhs_stage[k, row] = rhs_split[k, row]

    def inv_row(k):
        start(inv_copy, k)
        inv_stage[k, row] = inverses[k][...]

    def rhs_col(k):
        arrive(rhs_copy, k)
        start(rhs_z_copy, k)
        rhs_full[k, col] = rhs_stage[k, col]

    def inv_col(k):
        arrive(inv_copy, k)
        start(inv_z_copy, k)
        inv_full[k, col] = inv_stage[k, col]

    def split(k):
        for piece in range(grid):
            rhs_split[k, piece] = rights[k][:, piece * columns : (piece + 1) * columns]

    def right_side(k):
        arrive(rhs_z_copy, k)
        return rhs_full[k].reshape(width, columns)

    def apply_inverse(k, value):
        arrive(inv_z_copy, k)
        return dot(inv_full[k].reshape(width, width), value)

    def couple(level, k, value, first, send):
        arrive(coupling_copy, k)

        def body(at, carry):
            to = lax.rem(col + 1 + at, grid)
            product = dot(coupling[k, to], value)
            if not first:
                product = part[level, to] + product
            part[level, to] = product
            return carry

        if not send:
            lax.fori_loop(0, grid, body, 0)
            return

        def body_send(at, carry):
            body(at, carry)
            part_copy(level, at + 1).start()
            return carry

        lax.fori_loop(0, grid - 1, body_send, 0)
        body(grid - 1, 0)
        sent.extend(part_copy(level, step) for step in others)

    def reduced(level):
        total = part[level, col]
        for step in others:
            part_copy(level, step).wait_recv()
            total = total + arrived[level, lax.rem(col + grid - step, grid)]
        return total

    def emit(k, value):
        solved[k] = value.reshape(grid, rows, columns)
        start(out_z_copy, k)
        out_stage[k, col] = solved[k, col]

    def emit_row(k):
        arrive(out_z_copy, k)
        start(out_copy, k)
        out_full[k, row] = out_stage[k, row]

    split(0)
    mask(0)
    pl.semaphore_wait(barrier, 2 * (grid - 1) + layers - 1)
    rhs_row(0)
    inv_row(0)
    start(coupling_copy, 0)
    split(1)
    split(2)
    split(3)
    rhs_row(1)
    inv_row(1)
    rhs_col(0)
    inv_col(0)
    spread_coupling(1)
    spread_coupling(2)
    rhs_row(2)
    inv_row(2)
    rhs_row(3)
    inv_row(3)
    rhs_zero = right_side(0)
    rhs_col(1)
    inv_col(1)
    fore_zero = apply_inverse(0, rhs_zero)
    couple(0, 0, fore_zero, True, True)
    spread_coupling(3)
    spread_coupling(4)
    couple(1, 1, fore_zero, True, False)
    rhs_one = right_side(1)
    total = reduced(0)
    rhs_col(2)
    inv_col(2)
    fore_one = apply_inverse(1, rhs_one - total)
    couple(1, 2, fore_one, False, True)
    spread_coupling(5)
    spread_coupling(6)
    inv_row(7)
    inv_row(6)
    couple(2, 3, fore_zero, True, False)
    couple(2, 4, fore_one, False, False)
    rhs_two = right_side(2)
    total = reduced(1)
    rhs_col(3)
    inv_col(3)
    fore_two = apply_inverse(2, rhs_two - total)
    couple(2, 5, fore_two, False, True)
    spread_coupling(7)
    spread_coupling(8)
    inv_row(5)
    inv_row(4)
    inv_col(7)
    inv_col(6)
    spread_coupling(9)
    spread_coupling(10)
    spread_coupling(11)
    rhs_last = right_side(3)
    cross[0] = reduced(2)
    for step in range(1, layers):
        cross_copy(step).start()
    total = cross[0]
    for step in range(1, layers):
        cross_copy(step).wait_recv()
        total = total + cross[step]
    final_top = apply_inverse(7, apply_inverse(3, rhs_last - total))
    couple(3, 6, final_top, True, True)
    emit(3, final_top)
    couple(4, 7, final_top, True, False)
    residual = fore_two - reduced(3)
    inv_col(5)
    final_two = apply_inverse(6, residual)
    couple(4, 8, final_two, False, True)
    emit(2, final_two)
    emit_row(3)
    couple(5, 9, final_top, True, False)
    couple(5, 10, final_two, False, False)
    residual = fore_one - reduced(4)
    inv_col(4)
    final_one = apply_inverse(5, residual)
    couple(5, 11, final_one, False, True)
    emit(1, final_one)
    emit_row(2)
    final_zero = apply_inverse(4, fore_zero - reduced(5))
    emit(0, final_zero)
    emit_row(1)
    emit_row(0)

    for k in (3, 2, 1, 0):
        arrive(out_copy, k)
        for piece in range(grid):
            target = out_top if k == LEVELS else out_sub.at[k]
            target[:, piece * columns : (piece + 1) * columns] = out_full[k, piece]
    for copy in sent:
        copy.wait_send()
    for step in range(1, layers):
        cross_copy(step).wait_send()


def solve_in_kernel(
    layers,
    grid,
    rhs_sub,
    rhs_top,
    lower_inv_sub,
    lower_inv_top,
    upper_inv_sub,
    upper_inv_top,
    lower_sub,
    lower_top,
    upper_sub,
    upper_top,
    block_pattern,
):
    rows, count = rhs_top.shape[-2:]
    width = lower_inv_top.shape[-1]
    columns = count // grid
    levels = LEVELS + 1
    steps = 2 * LEVELS
    couplings = 4 * LEVELS
    f32 = jnp.float32

    def sub(array):
        return array.reshape((LEVELS,) + array.shape[-2:])

    def top(array):
        return array.reshape(array.shape[-2:])

    def sems(number, peers=grid):
        return pltpu.SemaphoreType.DMA((2, number, peers - 1))

    vmem = pl.BlockSpec(memory_space=pltpu.VMEM)
    out_sub, out_top = pl.pallas_call(
        functools.partial(kernel, layers, grid),
        out_shape=(
            jax.ShapeDtypeStruct((LEVELS, rows, count), f32),
            jax.ShapeDtypeStruct((rows, count), f32),
        ),
        in_specs=[pl.BlockSpec(memory_space=pltpu.SMEM)] + [vmem] * 10,
        out_specs=(vmem, vmem),
        scratch_shapes=[
            pltpu.VMEM((couplings, grid, width, width), f32),
            pltpu.VMEM((levels, grid, rows, columns), f32),
            pltpu.VMEM((levels, grid, rows, columns), f32),
            pltpu.VMEM((levels, grid, rows, columns), f32),
            pltpu.VMEM((2 * levels, grid, rows, width), f32),
            pltpu.VMEM((2 * levels, grid, rows, width), f32),
            pltpu.VMEM((steps, grid, width, columns), f32),
            pltpu.VMEM((steps, grid, width, columns), f32),
            pltpu.VMEM((levels, grid, rows, columns), f32),
            pltpu.VMEM((layers, width, columns), f32),
            pltpu.VMEM((levels, grid, rows, columns), f32),
            pltpu.VMEM((levels, grid, rows, columns), f32),
            sems(couplings),
            sems(levels),
            sems(levels),
            sems(2 * levels),
            sems(2 * levels),
            sems(steps),
            sems(1, layers),
            sems(levels),
            sems(levels),
        ],
        compiler_params=pltpu.CompilerParams(
            collective_id=0, has_side_effects=True, vmem_limit_bytes=48 * 2**20
        ),
        cost_estimate=pl.CostEstimate(
            flops=2 * couplings * grid * width * width * columns,
            bytes_accessed=4 * couplings * width * width,
            transcendentals=0,
        ),
    )(
        block_pattern.reshape(-1),
        sub(rhs_sub),
        top(rhs_top),
        sub(lower_inv_sub),
        top(lower_inv_top),
        sub(upper_inv_sub),
        top(upper_inv_top),
        sub(lower_sub),
        sub(lower_top),
        sub(upper_sub),
        sub(upper_top),
    )
    return out_sub.reshape(rhs_sub.shape), out_top.reshape(rhs_top.shape)


def broadcast(x, axis, root):
    mine = lax.axis_index(axis) == root
    return lax.psum(jnp.where(mine, x, jnp.zeros_like(x)), axis)


def couple(blocks, pattern, solution):
    weighted = solution[None] * pattern[:, :, None, None].astype(jnp.float32)
    return jnp.einsum("tsab,tsbn->tan", blocks, weighted, precision=HIGHEST)


def spread(whole_block):
    return broadcast(whole_block, "row", lax.axis_index("col"))


def on_device(
    rhs_sub,
    rhs_top,
    lower_inv_sub,
    lower_inv_top,
    upper_inv_sub,
    upper_inv_top,
    lower_sub,
    lower_top,
    upper_sub,
    upper_top,
    block_pattern,
):
    column = lax.axis_index("col")
    width_rows = rhs_top.shape[2]
    gathered = (
        lax.all_gather(lower_inv_sub, "col", axis=4, tiled=True),
        lax.all_gather(lower_inv_top, "col", axis=2, tiled=True),
        lax.all_gather(upper_inv_sub, "col", axis=4, tiled=True),
        lax.all_gather(upper_inv_top, "col", axis=2, tiled=True),
        lax.all_gather(rhs_sub, "col", axis=4, tiled=True),
        lax.all_gather(rhs_top, "col", axis=2, tiled=True),
    )
    lower_list = [gathered[0][0, level, :, 0] for level in range(3)] + [gathered[1][:, 0]]
    upper_list = [gathered[2][0, level, :, 0] for level in range(3)] + [gathered[3][:, 0]]
    right_sides = [gathered[4][0, level, :, 0] for level in range(3)] + [gathered[5][:, 0]]

    def solve(partial_value, right_side, inverse_full, top):
        if partial_value is None:
            residual = right_side
        elif top:
            residual = right_side - lax.psum(partial_value, ("layer", "col"))
        else:
            residual = right_side - lax.psum(partial_value, "col")
        return jnp.einsum("kab,kbn->kan", inverse_full, residual, precision=HIGHEST)

    def copy_out(solution):
        return spread(solution)

    def keep_rows(solution):
        return lax.dynamic_slice_in_dim(solution, column * width_rows, width_rows, 1)

    def blocks(array, pair):
        return array[0, pair, :, 0, :, 0]

    def pattern(kind, pair):
        return block_pattern[0, kind, pair, :, 0, :, 0]

    fore_zero = solve(None, right_sides[0], lower_list[0], False)
    copy_zero = copy_out(fore_zero)
    into_one = couple(blocks(lower_sub, 0), pattern(0, 0), copy_zero)
    into_two = couple(blocks(lower_sub, 1), pattern(0, 1), copy_zero)
    into_top = couple(blocks(lower_top, 0), pattern(1, 0), copy_zero)
    fore_one = solve(into_one, right_sides[1], lower_list[1], False)
    copy_one = copy_out(fore_one)
    into_two = into_two + couple(blocks(lower_sub, 2), pattern(0, 2), copy_one)
    into_top = into_top + couple(blocks(lower_top, 1), pattern(1, 1), copy_one)
    fore_two = solve(into_two, right_sides[2], lower_list[2], False)
    copy_two = copy_out(fore_two)
    into_top = into_top + couple(blocks(lower_top, 2), pattern(1, 2), copy_two)
    fore_top = solve(into_top, right_sides[3], lower_list[3], True)
    final_top = solve(None, fore_top, upper_list[3], False)
    down_top = copy_out(final_top)
    toward_two = couple(blocks(upper_top, 2), pattern(3, 2), down_top)
    toward_one = couple(blocks(upper_top, 1), pattern(3, 1), down_top)
    toward_zero = couple(blocks(upper_top, 0), pattern(3, 0), down_top)
    final_two = solve(toward_two, fore_two, upper_list[2], False)
    down_two = copy_out(final_two)
    toward_one = toward_one + couple(blocks(upper_sub, 2), pattern(2, 2), down_two)
    toward_zero = toward_zero + couple(blocks(upper_sub, 1), pattern(2, 1), down_two)
    final_one = solve(toward_one, fore_one, upper_list[1], False)
    down_one = copy_out(final_one)
    toward_zero = toward_zero + couple(blocks(upper_sub, 0), pattern(2, 0), down_one)
    final_zero = solve(toward_zero, fore_zero, upper_list[0], False)
    solution_sub = jnp.stack([keep_rows(final_zero), keep_rows(final_one), keep_rows(final_two)])[
        None, :, :, None
    ]
    solution_top = keep_rows(final_top)[:, None]
    return (solution_sub, solution_top)


def solution(mesh):
    placed = (
        P("layer", None, None, "row", "col", None),
        P(None, "row", "col", None),
        P("layer", None, None, "row", "col", None),
        P(None, "row", "col", None),
        P("layer", None, None, "row", "col", None),
        P(None, "row", "col", None),
        P("layer", None, None, "row", None, "col", None, None),
        P("layer", None, None, "row", None, "col", None, None),
        P("layer", None, None, "row", None, "col", None, None),
        P("layer", None, None, "row", None, "col", None, None),
        P("layer", None, None, None, "row", None, "col"),
    )
    layers, grid = mesh.shape["layer"], mesh.shape["row"]

    def choose(*arguments):
        rhs_sub, rhs_top, inverse = arguments[0], arguments[1], arguments[3]
        columns, width = rhs_top.shape[-1] // grid, inverse.shape[-1]
        square = mesh.shape["row"] == mesh.shape["col"] and rhs_sub.shape[2] == 1
        held = 4 * 4 * LEVELS * grid * width * width
        if square and grid > 1 and rhs_top.shape[-1] % (128 * grid) == 0 and held <= 2**24:
            return solve_in_kernel(layers, grid, *arguments)
        return on_device(*arguments)

    return jax.shard_map(
        choose,
        mesh=mesh,
        in_specs=placed,
        out_specs=(P("layer", None, None, "row", "col", None), P(None, "row", "col", None)),
        check_vma=False,
    )
```

```python
import functools
import jax
import jax.numpy as jnp
from jax import lax
from jax.experimental import pallas as pl
from jax.experimental.pallas import tpu as pltpu
from jax.sharding import PartitionSpec as P

HIGHEST = lax.Precision.HIGHEST
MESH = pl.DeviceIdType.MESH
LEVELS = 3


def halves(value):
    high = value.astype(jnp.bfloat16)
    return high, (value - high.astype(jnp.float32)).astype(jnp.bfloat16)


def pair(value):
    return jnp.concatenate(halves(value), axis=1)


def dot(a, paired):
    high, low = halves(a)
    both = jnp.dot(high, paired, preferred_element_type=jnp.float32)
    both = both + jnp.dot(low, paired, preferred_element_type=jnp.float32)
    columns = paired.shape[1] // 2
    return both[:, :columns] + both[:, columns:]


def kernel(
    layers,
    grid,
    pattern,
    rhs_sub,
    rhs_top,
    lower_inv_sub,
    lower_inv_top,
    upper_inv_sub,
    upper_inv_top,
    lower_sub,
    lower_top,
    upper_sub,
    upper_top,
    out_sub,
    out_top,
    own,
    own_rhs,
    coupling,
    rhs_split,
    rhs_stage,
    rhs_full,
    inv_stage,
    inv_full,
    part,
    arrived,
    solved,
    cross,
    out_stage,
    out_full,
    own_sem,
    own_rhs_sem,
    own_inv_sem,
    coupling_sem,
    rhs_sem,
    rhs_z_sem,
    inv_sem,
    inv_z_sem,
    part_sem,
    cross_sem,
    out_z_sem,
    out_sem,
):
    layer, row, col = lax.axis_index("layer"), lax.axis_index("row"), lax.axis_index("col")
    width = part.shape[2]
    columns = part.shape[3]
    others = range(1, grid)

    def ahead(me, step, count=grid):
        return lax.rem(me + step, count)

    barrier = pltpu.get_barrier_semaphore()
    for step in others:
        pl.semaphore_signal(barrier, inc=1, device_id=(layer, ahead(row, step), col), device_id_type=MESH)
        pl.semaphore_signal(barrier, inc=1, device_id=(layer, row, ahead(col, step)), device_id_type=MESH)
    for step in range(1, layers):
        pl.semaphore_signal(
            barrier, inc=1, device_id=(ahead(layer, step, layers), row, col), device_id_type=MESH
        )

    def remote(source, target, sems, index, step, device):
        return pltpu.make_async_remote_copy(
            src_ref=source,
            dst_ref=target,
            send_sem=sems.at[0, index, step - 1],
            recv_sem=sems.at[1, index, step - 1],
            device_id=device,
            device_id_type=MESH,
        )

    sources = (
        (lower_sub, 0, 0),
        (lower_sub, 1, 0),
        (lower_sub, 2, 0),
        (lower_top, 0, 1),
        (lower_top, 1, 1),
        (lower_top, 2, 1),
        (upper_top, 2, 3),
        (upper_top, 1, 3),
        (upper_sub, 2, 2),
        (upper_top, 0, 3),
        (upper_sub, 1, 2),
        (upper_sub, 0, 2),
    )
    inverses = tuple(lower_inv_sub.at[k] for k in range(LEVELS)) + (lower_inv_top,)
    inverses += tuple(upper_inv_sub.at[k] for k in range(LEVELS)) + (upper_inv_top,)
    rights = tuple(rhs_sub.at[k] for k in range(LEVELS)) + (rhs_top,)

    def own_copy(k):
        ref, at, _ = sources[k]
        return pltpu.make_async_copy(ref.at[at], own.at[k], own_sem.at[k])

    def own_rhs_copy(k):
        return pltpu.make_async_copy(rights[k], own_rhs.at[k], own_rhs_sem.at[k])

    def own_inv_copy(k):
        return pltpu.make_async_copy(inverses[k], inv_stage.at[k, row], own_inv_sem.at[k])

    own_rhs_copy(0).start()
    own_inv_copy(0).start()
    own_copy(0).start()
    for k in range(1, LEVELS + 1):
        own_rhs_copy(k).start()
        own_inv_copy(k).start()
    for k in range(1, len(sources)):
        own_copy(k).start()
    for k in range(LEVELS + 1, len(inverses)):
        own_inv_copy(k).start()

    def mask(k):
        _, at, kind = sources[k]
        own_copy(k).wait()
        coupling[k, row] = own[k] * pattern[kind * LEVELS + at].astype(jnp.float32)

    half = grid // 2
    beside = row + 1 - 2 * lax.rem(row, 2)
    above = lax.rem(row + half, grid)
    upper, lower = pl.ds(0, width // 2), pl.ds(width // 2, width // 2)

    def coupling_copy(k, step):
        to = (beside, above)[step - 1]
        return remote(coupling.at[k, row], coupling.at[k, row], coupling_sem, k, step, (layer, to, col))

    def relay_copy(k, step):
        come, to, part_rows = ((beside, above, upper), (above, beside, lower))[step - 1]
        block = coupling.at[k, come, part_rows]
        return remote(block, block, coupling_sem, k, step + 2, (layer, to, col))

    def relay(k):
        for step in (1, 2):
            coupling_copy(k, step).wait_recv()
            copy = relay_copy(k, step)
            copy.start()
            sent.append(copy)

    def rhs_copy(k, step):
        to = ahead(row, step)
        return remote(rhs_split.at[k, to], rhs_stage.at[k, row], rhs_sem, k, step, (layer, to, col))

    def inv_copy(k, step):
        return remote(inv_stage.at[k, row], inv_stage.at[k, row], inv_sem, k, step, (layer, ahead(row, step), col))

    def rhs_z_copy(k, step):
        to = ahead(col, step)
        return remote(rhs_stage.at[k, to], rhs_full.at[k, col], rhs_z_sem, k, step, (layer, row, to))

    def inv_z_copy(k, step):
        to = ahead(col, step)
        return remote(inv_stage.at[k, to], inv_full.at[k, col], inv_z_sem, k, step, (layer, row, to))

    def part_copy(k, step):
        to = ahead(col, step)
        return remote(part.at[k, to], arrived.at[k, col], part_sem, k, step, (layer, row, to))

    def cross_copy(step):
        return remote(
            cross.at[0], cross.at[step], cross_sem, 0, step, (ahead(layer, step, layers), row, col)
        )

    rows = width // grid

    def out_z_copy(k, step):
        to = ahead(col, step)
        return remote(solved.at[k, to], out_stage.at[k, col], out_z_sem, k, step, (layer, row, to))

    def out_copy(k, step):
        to = ahead(row, step)
        return remote(out_stage.at[k, to], out_full.at[k, row], out_sem, k, step, (layer, to, col))

    sent = []

    def start(make, k):
        for step in others:
            copy = make(k, step)
            copy.start()
            sent.append(copy)

    def arrive(make, k):
        for step in others:
            make(k, step).wait_recv()

    def spread_coupling(k):
        mask(k)
        for step in (1, 2):
            copy = coupling_copy(k, step)
            copy.start()
            sent.append(copy)

    def rhs_row(k):
        start(rhs_copy, k)
        rhs_stage[k, row] = rhs_split[k, row]

    def inv_row(k):
        own_inv_copy(k).wait()
        start(inv_copy, k)

    def rhs_col(k):
        arrive(rhs_copy, k)
        start(rhs_z_copy, k)
        rhs_full[k, col] = rhs_stage[k, col]

    def inv_col(k):
        arrive(inv_copy, k)
        start(inv_z_copy, k)
        inv_full[k, col] = inv_stage[k, col]

    def split(k):
        own_rhs_copy(k).wait()
        for piece in range(grid):
            rhs_split[k, piece] = own_rhs[k, :, piece * columns : (piece + 1) * columns]

    def right_side(k):
        arrive(rhs_z_copy, k)
        return rhs_full[k].reshape(width, columns)

    def apply_inverse(k, value):
        arrive(inv_z_copy, k)
        return dot(inv_full[k].reshape(width, width), pair(value))

    def couple(level, k, value, first, send):
        for step in (1, 2):
            relay_copy(k, step).wait_recv()

        def body(at, carry):
            to = lax.rem(col + 1 + at, grid)
            product = dot(coupling[k, to], value)
            if not first:
                product = part[level, to] + product
            part[level, to] = product
            return carry

        if not send:
            lax.fori_loop(0, grid, body, 0)
            return

        def body_send(at, carry):
            body(at, carry)
            part_copy(level, at + 1).start()
            return carry

        lax.fori_loop(0, grid - 1, body_send, 0)
        body(grid - 1, 0)
        sent.extend(part_copy(level, step) for step in others)

    def reduced(level):
        total = part[level, col]
        for step in others:
            part_copy(level, step).wait_recv()
            total = total + arrived[level, lax.rem(col + grid - step, grid)]
        return total

    def emit(k, value):
        solved[k] = value.reshape(grid, rows, columns)
        start(out_z_copy, k)
        out_stage[k, col] = solved[k, col]

    def emit_row(k):
        arrive(out_z_copy, k)
        start(out_copy, k)
        out_full[k, row] = out_stage[k, row]

    pl.semaphore_wait(barrier, 2 * (grid - 1) + layers - 1)
    split(0)
    rhs_row(0)
    inv_row(0)
    spread_coupling(0)
    for k in range(1, LEVELS + 1):
        split(k)
    rhs_row(1)
    inv_row(1)
    spread_coupling(1)
    rhs_col(0)
    inv_col(0)
    spread_coupling(2)
    relay(0)
    rhs_col(1)
    inv_col(1)
    rhs_row(2)
    inv_row(2)
    spread_coupling(3)
    fore_zero = apply_inverse(0, right_side(0))
    fore_zero_pair = pair(fore_zero)
    couple(0, 0, fore_zero_pair, True, True)
    relay(1)
    spread_coupling(4)
    relay(2)
    spread_coupling(5)
    rhs_row(3)
    inv_row(3)
    couple(1, 1, fore_zero_pair, True, False)
    total = reduced(0)
    rhs_col(2)
    inv_col(2)
    fore_one = apply_inverse(1, right_side(1) - total)
    fore_one_pair = pair(fore_one)
    couple(1, 2, fore_one_pair, False, True)
    relay(3)
    spread_coupling(6)
    inv_row(7)
    inv_row(6)
    relay(4)
    spread_coupling(7)
    couple(2, 3, fore_zero_pair, True, False)
    rhs_col(3)
    inv_col(3)
    couple(2, 4, fore_one_pair, False, False)
    total = reduced(1)
    relay(5)
    fore_two = apply_inverse(2, right_side(2) - total)
    spread_coupling(8)
    couple(2, 5, pair(fore_two), False, True)
    relay(6)
    spread_coupling(9)
    inv_row(5)
    inv_row(4)
    inv_col(7)
    inv_col(6)
    relay(7)
    spread_coupling(10)
    rhs_last = right_side(3)
    cross[0] = reduced(2)
    for step in range(1, layers):
        cross_copy(step).start()
    total = cross[0]
    for step in range(1, layers):
        cross_copy(step).wait_recv()
        total = total + cross[step]
    final_top = apply_inverse(7, apply_inverse(3, rhs_last - total))
    final_top_pair = pair(final_top)
    couple(3, 6, final_top_pair, True, True)
    emit(3, final_top)
    relay(8)
    spread_coupling(11)
    couple(4, 7, final_top_pair, True, False)
    relay(9)
    residual = fore_two - reduced(3)
    inv_col(5)
    final_two = apply_inverse(6, residual)
    final_two_pair = pair(final_two)
    couple(4, 8, final_two_pair, False, True)
    emit(2, final_two)
    emit_row(3)
    relay(10)
    couple(5, 9, final_top_pair, True, False)
    relay(11)
    couple(5, 10, final_two_pair, False, False)
    residual = fore_one - reduced(4)
    inv_col(4)
    final_one = apply_inverse(5, residual)
    couple(5, 11, pair(final_one), False, True)
    emit(1, final_one)
    emit_row(2)
    final_zero = apply_inverse(4, fore_zero - reduced(5))
    emit(0, final_zero)
    emit_row(1)
    emit_row(0)

    for k in (3, 2, 1, 0):
        arrive(out_copy, k)
        for piece in range(grid):
            target = out_top if k == LEVELS else out_sub.at[k]
            target[:, piece * columns : (piece + 1) * columns] = out_full[k, piece]
    for copy in sent:
        copy.wait_send()
    for step in range(1, layers):
        cross_copy(step).wait_send()


def solve_in_kernel(
    layers,
    grid,
    rhs_sub,
    rhs_top,
    lower_inv_sub,
    lower_inv_top,
    upper_inv_sub,
    upper_inv_top,
    lower_sub,
    lower_top,
    upper_sub,
    upper_top,
    block_pattern,
):
    rows, count = rhs_top.shape[-2:]
    width = lower_inv_top.shape[-1]
    columns = count // grid
    levels = LEVELS + 1
    steps = 2 * LEVELS
    couplings = 4 * LEVELS
    f32 = jnp.float32

    def sub(array):
        return array.reshape((LEVELS,) + array.shape[-2:])

    def top(array):
        return array.reshape(array.shape[-2:])

    def sems(number, peers=grid):
        return pltpu.SemaphoreType.DMA((2, number, peers - 1))

    vmem = pl.BlockSpec(memory_space=pltpu.VMEM)
    out_sub, out_top = pl.pallas_call(
        functools.partial(kernel, layers, grid),
        out_shape=(
            jax.ShapeDtypeStruct((LEVELS, rows, count), f32),
            jax.ShapeDtypeStruct((rows, count), f32),
        ),
        in_specs=[pl.BlockSpec(memory_space=pltpu.SMEM)] + [pl.BlockSpec(memory_space=pl.ANY)] * 10,
        out_specs=(vmem, vmem),
        scratch_shapes=[
            pltpu.VMEM((couplings, width, width), f32),
            pltpu.VMEM((levels, rows, count), f32),
            pltpu.VMEM((couplings, grid, width, width), f32),
            pltpu.VMEM((levels, grid, rows, columns), f32),
            pltpu.VMEM((levels, grid, rows, columns), f32),
            pltpu.VMEM((levels, grid, rows, columns), f32),
            pltpu.VMEM((2 * levels, grid, rows, width), f32),
            pltpu.VMEM((2 * levels, grid, rows, width), f32),
            pltpu.VMEM((steps, grid, width, columns), f32),
            pltpu.VMEM((steps, grid, width, columns), f32),
            pltpu.VMEM((levels, grid, rows, columns), f32),
            pltpu.VMEM((layers, width, columns), f32),
            pltpu.VMEM((levels, grid, rows, columns), f32),
            pltpu.VMEM((levels, grid, rows, columns), f32),
            pltpu.SemaphoreType.DMA((couplings,)),
            pltpu.SemaphoreType.DMA((levels,)),
            pltpu.SemaphoreType.DMA((2 * levels,)),
            pltpu.SemaphoreType.DMA((2, couplings, 4)),
            sems(levels),
            sems(levels),
            sems(2 * levels),
            sems(2 * levels),
            sems(steps),
            sems(1, layers),
            sems(levels),
            sems(levels),
        ],
        compiler_params=pltpu.CompilerParams(
            collective_id=0, has_side_effects=True, vmem_limit_bytes=48 * 2**20
        ),
        cost_estimate=pl.CostEstimate(
            flops=2 * couplings * grid * width * width * columns,
            bytes_accessed=4 * couplings * width * width,
            transcendentals=0,
        ),
    )(
        block_pattern.reshape(-1),
        sub(rhs_sub),
        top(rhs_top),
        sub(lower_inv_sub),
        top(lower_inv_top),
        sub(upper_inv_sub),
        top(upper_inv_top),
        sub(lower_sub),
        sub(lower_top),
        sub(upper_sub),
        sub(upper_top),
    )
    return out_sub.reshape(rhs_sub.shape), out_top.reshape(rhs_top.shape)


def broadcast(x, axis, root):
    mine = lax.axis_index(axis) == root
    return lax.psum(jnp.where(mine, x, jnp.zeros_like(x)), axis)


def couple(blocks, pattern, solution):
    weighted = solution[None] * pattern[:, :, None, None].astype(jnp.float32)
    return jnp.einsum("tsab,tsbn->tan", blocks, weighted, precision=HIGHEST)


def spread(whole_block):
    return broadcast(whole_block, "row", lax.axis_index("col"))


def on_device(
    rhs_sub,
    rhs_top,
    lower_inv_sub,
    lower_inv_top,
    upper_inv_sub,
    upper_inv_top,
    lower_sub,
    lower_top,
    upper_sub,
    upper_top,
    block_pattern,
):
    column = lax.axis_index("col")
    width_rows = rhs_top.shape[2]
    gathered = (
        lax.all_gather(lower_inv_sub, "col", axis=4, tiled=True),
        lax.all_gather(lower_inv_top, "col", axis=2, tiled=True),
        lax.all_gather(upper_inv_sub, "col", axis=4, tiled=True),
        lax.all_gather(upper_inv_top, "col", axis=2, tiled=True),
        lax.all_gather(rhs_sub, "col", axis=4, tiled=True),
        lax.all_gather(rhs_top, "col", axis=2, tiled=True),
    )
    lower_list = [gathered[0][0, level, :, 0] for level in range(3)] + [gathered[1][:, 0]]
    upper_list = [gathered[2][0, level, :, 0] for level in range(3)] + [gathered[3][:, 0]]
    right_sides = [gathered[4][0, level, :, 0] for level in range(3)] + [gathered[5][:, 0]]

    def solve(partial_value, right_side, inverse_full, top):
        if partial_value is None:
            residual = right_side
        elif top:
            residual = right_side - lax.psum(partial_value, ("layer", "col"))
        else:
            residual = right_side - lax.psum(partial_value, "col")
        return jnp.einsum("kab,kbn->kan", inverse_full, residual, precision=HIGHEST)

    def copy_out(solution):
        return spread(solution)

    def keep_rows(solution):
        return lax.dynamic_slice_in_dim(solution, column * width_rows, width_rows, 1)

    def blocks(array, pair):
        return array[0, pair, :, 0, :, 0]

    def pattern(kind, pair):
        return block_pattern[0, kind, pair, :, 0, :, 0]

    fore_zero = solve(None, right_sides[0], lower_list[0], False)
    copy_zero = copy_out(fore_zero)
    into_one = couple(blocks(lower_sub, 0), pattern(0, 0), copy_zero)
    into_two = couple(blocks(lower_sub, 1), pattern(0, 1), copy_zero)
    into_top = couple(blocks(lower_top, 0), pattern(1, 0), copy_zero)
    fore_one = solve(into_one, right_sides[1], lower_list[1], False)
    copy_one = copy_out(fore_one)
    into_two = into_two + couple(blocks(lower_sub, 2), pattern(0, 2), copy_one)
    into_top = into_top + couple(blocks(lower_top, 1), pattern(1, 1), copy_one)
    fore_two = solve(into_two, right_sides[2], lower_list[2], False)
    copy_two = copy_out(fore_two)
    into_top = into_top + couple(blocks(lower_top, 2), pattern(1, 2), copy_two)
    fore_top = solve(into_top, right_sides[3], lower_list[3], True)
    final_top = solve(None, fore_top, upper_list[3], False)
    down_top = copy_out(final_top)
    toward_two = couple(blocks(upper_top, 2), pattern(3, 2), down_top)
    toward_one = couple(blocks(upper_top, 1), pattern(3, 1), down_top)
    toward_zero = couple(blocks(upper_top, 0), pattern(3, 0), down_top)
    final_two = solve(toward_two, fore_two, upper_list[2], False)
    down_two = copy_out(final_two)
    toward_one = toward_one + couple(blocks(upper_sub, 2), pattern(2, 2), down_two)
    toward_zero = toward_zero + couple(blocks(upper_sub, 1), pattern(2, 1), down_two)
    final_one = solve(toward_one, fore_one, upper_list[1], False)
    down_one = copy_out(final_one)
    toward_zero = toward_zero + couple(blocks(upper_sub, 0), pattern(2, 0), down_one)
    final_zero = solve(toward_zero, fore_zero, upper_list[0], False)
    solution_sub = jnp.stack([keep_rows(final_zero), keep_rows(final_one), keep_rows(final_two)])[
        None, :, :, None
    ]
    solution_top = keep_rows(final_top)[:, None]
    return (solution_sub, solution_top)


def solution(mesh):
    placed = (
        P("layer", None, None, "row", "col", None),
        P(None, "row", "col", None),
        P("layer", None, None, "row", "col", None),
        P(None, "row", "col", None),
        P("layer", None, None, "row", "col", None),
        P(None, "row", "col", None),
        P("layer", None, None, "row", None, "col", None, None),
        P("layer", None, None, "row", None, "col", None, None),
        P("layer", None, None, "row", None, "col", None, None),
        P("layer", None, None, "row", None, "col", None, None),
        P("layer", None, None, None, "row", None, "col"),
    )
    layers, grid = mesh.shape["layer"], mesh.shape["row"]

    def choose(*arguments):
        rhs_sub, rhs_top, inverse = arguments[0], arguments[1], arguments[3]
        columns, width = rhs_top.shape[-1] // grid, inverse.shape[-1]
        square = mesh.shape["row"] == mesh.shape["col"] and rhs_sub.shape[2] == 1
        held = 4 * 4 * LEVELS * grid * width * width
        if square and grid == 4 and rhs_top.shape[-1] % (128 * grid) == 0 and held <= 2**24:
            return solve_in_kernel(layers, grid, *arguments)
        return on_device(*arguments)

    return jax.shard_map(
        choose,
        mesh=mesh,
        in_specs=placed,
        out_specs=(P("layer", None, None, "row", "col", None), P(None, "row", "col", None)),
        check_vma=False,
    )
```

```python
import functools
import jax
import jax.numpy as jnp
from jax import lax
from jax.experimental import pallas as pl
from jax.experimental.pallas import tpu as pltpu
from jax.sharding import PartitionSpec as P

HIGHEST = lax.Precision.HIGHEST
MESH = pl.DeviceIdType.MESH
LEVELS = 3


def halves(value):
    high = value.astype(jnp.bfloat16)
    return high, (value - high.astype(jnp.float32)).astype(jnp.bfloat16)


def pair(value):
    return jnp.concatenate(halves(value), axis=1)


def dot(a, paired):
    high, low = halves(a)
    both = jnp.dot(high, paired, preferred_element_type=jnp.float32)
    both = both + jnp.dot(low, paired, preferred_element_type=jnp.float32)
    columns = paired.shape[1] // 2
    return both[:, :columns] + both[:, columns:]


def kernel(
    layers,
    grid,
    pattern,
    rhs_sub,
    rhs_top,
    lower_inv_sub,
    lower_inv_top,
    upper_inv_sub,
    upper_inv_top,
    lower_sub,
    lower_top,
    upper_sub,
    upper_top,
    out_sub,
    out_top,
    own,
    own_rhs,
    coupling,
    rhs_split,
    rhs_stage,
    rhs_full,
    inv_stage,
    inv_full,
    part,
    given,
    arrived,
    solved,
    cross,
    out_stage,
    out_full,
    own_sem,
    own_rhs_sem,
    own_inv_sem,
    coupling_sem,
    rhs_sem,
    rhs_z_sem,
    inv_sem,
    inv_z_sem,
    part_sem,
    cross_sem,
    out_z_sem,
    out_sem,
):
    layer, row, col = lax.axis_index("layer"), lax.axis_index("row"), lax.axis_index("col")
    width = part.shape[2]
    columns = part.shape[3]
    others = range(1, grid)

    def ahead(me, step, count=grid):
        return lax.rem(me + step, count)

    barrier = pltpu.get_barrier_semaphore()
    for step in others:
        pl.semaphore_signal(barrier, inc=1, device_id=(layer, ahead(row, step), col), device_id_type=MESH)
        pl.semaphore_signal(barrier, inc=1, device_id=(layer, row, ahead(col, step)), device_id_type=MESH)
    for step in range(1, layers):
        pl.semaphore_signal(
            barrier, inc=1, device_id=(ahead(layer, step, layers), row, col), device_id_type=MESH
        )

    def remote(source, target, sems, index, step, device):
        return pltpu.make_async_remote_copy(
            src_ref=source,
            dst_ref=target,
            send_sem=sems.at[0, index, step - 1],
            recv_sem=sems.at[1, index, step - 1],
            device_id=device,
            device_id_type=MESH,
        )

    sources = (
        (lower_sub, 0, 0),
        (lower_sub, 1, 0),
        (lower_sub, 2, 0),
        (lower_top, 0, 1),
        (lower_top, 1, 1),
        (lower_top, 2, 1),
        (upper_top, 2, 3),
        (upper_top, 1, 3),
        (upper_sub, 2, 2),
        (upper_top, 0, 3),
        (upper_sub, 1, 2),
        (upper_sub, 0, 2),
    )
    inverses = tuple(lower_inv_sub.at[k] for k in range(LEVELS)) + (lower_inv_top,)
    inverses += tuple(upper_inv_sub.at[k] for k in range(LEVELS)) + (upper_inv_top,)
    rights = tuple(rhs_sub.at[k] for k in range(LEVELS)) + (rhs_top,)

    def own_copy(k):
        ref, at, _ = sources[k]
        return pltpu.make_async_copy(ref.at[at], own.at[k], own_sem.at[k])

    def own_rhs_copy(k):
        return pltpu.make_async_copy(rights[k], own_rhs.at[k], own_rhs_sem.at[k])

    def own_inv_copy(k):
        return pltpu.make_async_copy(inverses[k], inv_stage.at[k, row], own_inv_sem.at[k])

    own_rhs_copy(0).start()
    own_inv_copy(0).start()
    own_copy(0).start()
    for k in range(1, LEVELS + 1):
        own_rhs_copy(k).start()
        own_inv_copy(k).start()
    for k in range(1, len(sources)):
        own_copy(k).start()
    for k in range(LEVELS + 1, len(inverses)):
        own_inv_copy(k).start()

    def mask(k):
        _, at, kind = sources[k]
        own_copy(k).wait()
        coupling[k, row] = own[k] * pattern[kind * LEVELS + at].astype(jnp.float32)

    half = grid // 2
    beside = row + 1 - 2 * lax.rem(row, 2)
    above = lax.rem(row + half, grid)
    upper, lower = pl.ds(0, width // 2), pl.ds(width // 2, width // 2)

    def coupling_copy(k, step):
        to = (beside, above)[step - 1]
        return remote(coupling.at[k, row], coupling.at[k, row], coupling_sem, k, step, (layer, to, col))

    def relay_copy(k, step):
        come, to, part_rows = ((beside, above, upper), (above, beside, lower))[step - 1]
        block = coupling.at[k, come, part_rows]
        return remote(block, block, coupling_sem, k, step + 2, (layer, to, col))

    def relay(k):
        for step in (1, 2):
            coupling_copy(k, step).wait_recv()
            copy = relay_copy(k, step)
            copy.start()
            sent.append(copy)

    def rhs_copy(k, step):
        to = ahead(row, step)
        return remote(rhs_split.at[k, to], rhs_stage.at[k, row], rhs_sem, k, step, (layer, to, col))

    def inv_copy(k, step):
        return remote(inv_stage.at[k, row], inv_stage.at[k, row], inv_sem, k, step, (layer, ahead(row, step), col))

    def rhs_z_copy(k, step):
        to = ahead(col, step)
        return remote(rhs_stage.at[k, to], rhs_full.at[k, col], rhs_z_sem, k, step, (layer, row, to))

    def inv_z_copy(k, step):
        to = ahead(col, step)
        return remote(inv_stage.at[k, to], inv_full.at[k, col], inv_z_sem, k, step, (layer, row, to))

    mate = col + 1 - 2 * lax.rem(col, 2)
    keep, give = lax.rem(col + half, grid), lax.rem(mate + half, grid)

    def give_copy(k):
        return remote(part.at[k, give], given.at[k], part_sem, k, 1, (layer, row, mate))

    def near_copy(k):
        return remote(part.at[k, mate], arrived.at[k, 0], part_sem, k, 2, (layer, row, mate))

    def far_copy(k):
        return remote(part.at[k, keep], arrived.at[k, 1], part_sem, k, 3, (layer, row, keep))

    def cross_copy(step):
        return remote(
            cross.at[0], cross.at[step], cross_sem, 0, step, (ahead(layer, step, layers), row, col)
        )

    rows = width // grid

    def out_z_copy(k, step):
        to = ahead(col, step)
        return remote(solved.at[k, to], out_stage.at[k, col], out_z_sem, k, step, (layer, row, to))

    def out_copy(k, step):
        to = ahead(row, step)
        return remote(out_stage.at[k, to], out_full.at[k, row], out_sem, k, step, (layer, to, col))

    sent = []

    def start(make, k):
        for step in others:
            copy = make(k, step)
            copy.start()
            sent.append(copy)

    def arrive(make, k):
        for step in others:
            make(k, step).wait_recv()

    def spread_coupling(k):
        mask(k)
        for step in (1, 2):
            copy = coupling_copy(k, step)
            copy.start()
            sent.append(copy)

    def rhs_row(k):
        start(rhs_copy, k)
        rhs_stage[k, row] = rhs_split[k, row]

    def inv_row(k):
        own_inv_copy(k).wait()
        start(inv_copy, k)

    def rhs_col(k):
        arrive(rhs_copy, k)
        start(rhs_z_copy, k)
        rhs_full[k, col] = rhs_stage[k, col]

    def inv_col(k):
        arrive(inv_copy, k)
        start(inv_z_copy, k)
        inv_full[k, col] = inv_stage[k, col]

    def split(k):
        own_rhs_copy(k).wait()
        for piece in range(grid):
            rhs_split[k, piece] = own_rhs[k, :, piece * columns : (piece + 1) * columns]

    def right_side(k):
        arrive(rhs_z_copy, k)
        return rhs_full[k].reshape(width, columns)

    def apply_inverse(k, value):
        arrive(inv_z_copy, k)
        return dot(inv_full[k].reshape(width, width), pair(value))

    def couple(level, k, value, first, send):
        for step in (1, 2):
            relay_copy(k, step).wait_recv()

        def add(to):
            product = dot(coupling[k, to], value)
            if not first:
                product = part[level, to] + product
            part[level, to] = product

        if not send:

            def body(to, carry):
                add(to)
                return carry

            lax.fori_loop(0, grid, body, 0)
            return

        add(give)
        give_copy(level).start()
        add(mate)
        near_copy(level).start()
        add(keep)
        give_copy(level).wait_recv()
        part[level, keep] = part[level, keep] + given[level]
        far_copy(level).start()
        add(col)
        sent.extend((give_copy(level), near_copy(level), far_copy(level)))

    def reduced(level):
        near_copy(level).wait_recv()
        total = part[level, col] + arrived[level, 0]
        far_copy(level).wait_recv()
        return total + arrived[level, 1]

    def emit(k, value):
        solved[k] = value.reshape(grid, rows, columns)
        start(out_z_copy, k)
        out_stage[k, col] = solved[k, col]

    def emit_row(k):
        arrive(out_z_copy, k)
        start(out_copy, k)
        out_full[k, row] = out_stage[k, row]

    pl.semaphore_wait(barrier, 2 * (grid - 1) + layers - 1)
    split(0)
    rhs_row(0)
    inv_row(0)
    spread_coupling(0)
    for k in range(1, LEVELS + 1):
        split(k)
    rhs_row(1)
    inv_row(1)
    spread_coupling(1)
    rhs_col(0)
    inv_col(0)
    spread_coupling(2)
    relay(0)
    rhs_col(1)
    inv_col(1)
    rhs_row(2)
    inv_row(2)
    spread_coupling(3)
    fore_zero = apply_inverse(0, right_side(0))
    fore_zero_pair = pair(fore_zero)
    couple(0, 0, fore_zero_pair, True, True)
    relay(1)
    spread_coupling(4)
    relay(2)
    spread_coupling(5)
    rhs_row(3)
    inv_row(3)
    couple(1, 1, fore_zero_pair, True, False)
    total = reduced(0)
    rhs_col(2)
    inv_col(2)
    fore_one = apply_inverse(1, right_side(1) - total)
    fore_one_pair = pair(fore_one)
    couple(1, 2, fore_one_pair, False, True)
    relay(3)
    spread_coupling(6)
    inv_row(7)
    inv_row(6)
    relay(4)
    spread_coupling(7)
    couple(2, 3, fore_zero_pair, True, False)
    rhs_col(3)
    inv_col(3)
    couple(2, 4, fore_one_pair, False, False)
    total = reduced(1)
    relay(5)
    fore_two = apply_inverse(2, right_side(2) - total)
    spread_coupling(8)
    couple(2, 5, pair(fore_two), False, True)
    relay(6)
    spread_coupling(9)
    inv_row(5)
    inv_row(4)
    inv_col(7)
    inv_col(6)
    relay(7)
    spread_coupling(10)
    rhs_last = right_side(3)
    cross[0] = reduced(2)
    for step in range(1, layers):
        cross_copy(step).start()
    total = cross[0]
    for step in range(1, layers):
        cross_copy(step).wait_recv()
        total = total + cross[step]
    final_top = apply_inverse(7, apply_inverse(3, rhs_last - total))
    final_top_pair = pair(final_top)
    couple(3, 6, final_top_pair, True, True)
    emit(3, final_top)
    relay(8)
    spread_coupling(11)
    couple(4, 7, final_top_pair, True, False)
    relay(9)
    residual = fore_two - reduced(3)
    inv_col(5)
    final_two = apply_inverse(6, residual)
    final_two_pair = pair(final_two)
    couple(4, 8, final_two_pair, False, True)
    emit(2, final_two)
    emit_row(3)
    relay(10)
    couple(5, 9, final_top_pair, True, False)
    relay(11)
    couple(5, 10, final_two_pair, False, False)
    residual = fore_one - reduced(4)
    inv_col(4)
    final_one = apply_inverse(5, residual)
    couple(5, 11, pair(final_one), False, True)
    emit(1, final_one)
    emit_row(2)
    final_zero = apply_inverse(4, fore_zero - reduced(5))
    emit(0, final_zero)
    emit_row(1)
    emit_row(0)

    for k in (3, 2, 1, 0):
        arrive(out_copy, k)
        for piece in range(grid):
            target = out_top if k == LEVELS else out_sub.at[k]
            target[:, piece * columns : (piece + 1) * columns] = out_full[k, piece]
    for copy in sent:
        copy.wait_send()
    for step in range(1, layers):
        cross_copy(step).wait_send()


def solve_in_kernel(
    layers,
    grid,
    rhs_sub,
    rhs_top,
    lower_inv_sub,
    lower_inv_top,
    upper_inv_sub,
    upper_inv_top,
    lower_sub,
    lower_top,
    upper_sub,
    upper_top,
    block_pattern,
):
    rows, count = rhs_top.shape[-2:]
    width = lower_inv_top.shape[-1]
    columns = count // grid
    levels = LEVELS + 1
    steps = 2 * LEVELS
    couplings = 4 * LEVELS
    f32 = jnp.float32

    def sub(array):
        return array.reshape((LEVELS,) + array.shape[-2:])

    def top(array):
        return array.reshape(array.shape[-2:])

    def sems(number, peers=grid):
        return pltpu.SemaphoreType.DMA((2, number, peers - 1))

    vmem = pl.BlockSpec(memory_space=pltpu.VMEM)
    out_sub, out_top = pl.pallas_call(
        functools.partial(kernel, layers, grid),
        out_shape=(
            jax.ShapeDtypeStruct((LEVELS, rows, count), f32),
            jax.ShapeDtypeStruct((rows, count), f32),
        ),
        in_specs=[pl.BlockSpec(memory_space=pltpu.SMEM)] + [pl.BlockSpec(memory_space=pltpu.HBM)] * 10,
        out_specs=(vmem, vmem),
        scratch_shapes=[
            pltpu.VMEM((couplings, width, width), f32),
            pltpu.VMEM((levels, rows, count), f32),
            pltpu.VMEM((couplings, grid, width, width), f32),
            pltpu.VMEM((levels, grid, rows, columns), f32),
            pltpu.VMEM((levels, grid, rows, columns), f32),
            pltpu.VMEM((levels, grid, rows, columns), f32),
            pltpu.VMEM((2 * levels, grid, rows, width), f32),
            pltpu.VMEM((2 * levels, grid, rows, width), f32),
            pltpu.VMEM((steps, grid, width, columns), f32),
            pltpu.VMEM((steps, width, columns), f32),
            pltpu.VMEM((steps, 2, width, columns), f32),
            pltpu.VMEM((levels, grid, rows, columns), f32),
            pltpu.VMEM((layers, width, columns), f32),
            pltpu.VMEM((levels, grid, rows, columns), f32),
            pltpu.VMEM((levels, grid, rows, columns), f32),
            pltpu.SemaphoreType.DMA((couplings,)),
            pltpu.SemaphoreType.DMA((levels,)),
            pltpu.SemaphoreType.DMA((2 * levels,)),
            pltpu.SemaphoreType.DMA((2, couplings, 4)),
            sems(levels),
            sems(levels),
            sems(2 * levels),
            sems(2 * levels),
            sems(steps),
            sems(1, layers),
            sems(levels),
            sems(levels),
        ],
        compiler_params=pltpu.CompilerParams(
            collective_id=0, has_side_effects=True, vmem_limit_bytes=48 * 2**20
        ),
        cost_estimate=pl.CostEstimate(
            flops=2 * couplings * grid * width * width * columns,
            bytes_accessed=4 * couplings * width * width,
            transcendentals=0,
        ),
    )(
        block_pattern.reshape(-1),
        sub(rhs_sub),
        top(rhs_top),
        sub(lower_inv_sub),
        top(lower_inv_top),
        sub(upper_inv_sub),
        top(upper_inv_top),
        sub(lower_sub),
        sub(lower_top),
        sub(upper_sub),
        sub(upper_top),
    )
    return out_sub.reshape(rhs_sub.shape), out_top.reshape(rhs_top.shape)


def broadcast(x, axis, root):
    mine = lax.axis_index(axis) == root
    return lax.psum(jnp.where(mine, x, jnp.zeros_like(x)), axis)


def couple(blocks, pattern, solution):
    weighted = solution[None] * pattern[:, :, None, None].astype(jnp.float32)
    return jnp.einsum("tsab,tsbn->tan", blocks, weighted, precision=HIGHEST)


def spread(whole_block):
    return broadcast(whole_block, "row", lax.axis_index("col"))


def on_device(
    rhs_sub,
    rhs_top,
    lower_inv_sub,
    lower_inv_top,
    upper_inv_sub,
    upper_inv_top,
    lower_sub,
    lower_top,
    upper_sub,
    upper_top,
    block_pattern,
):
    column = lax.axis_index("col")
    width_rows = rhs_top.shape[2]
    gathered = (
        lax.all_gather(lower_inv_sub, "col", axis=4, tiled=True),
        lax.all_gather(lower_inv_top, "col", axis=2, tiled=True),
        lax.all_gather(upper_inv_sub, "col", axis=4, tiled=True),
        lax.all_gather(upper_inv_top, "col", axis=2, tiled=True),
        lax.all_gather(rhs_sub, "col", axis=4, tiled=True),
        lax.all_gather(rhs_top, "col", axis=2, tiled=True),
    )
    lower_list = [gathered[0][0, level, :, 0] for level in range(3)] + [gathered[1][:, 0]]
    upper_list = [gathered[2][0, level, :, 0] for level in range(3)] + [gathered[3][:, 0]]
    right_sides = [gathered[4][0, level, :, 0] for level in range(3)] + [gathered[5][:, 0]]

    def solve(partial_value, right_side, inverse_full, top):
        if partial_value is None:
            residual = right_side
        elif top:
            residual = right_side - lax.psum(partial_value, ("layer", "col"))
        else:
            residual = right_side - lax.psum(partial_value, "col")
        return jnp.einsum("kab,kbn->kan", inverse_full, residual, precision=HIGHEST)

    def copy_out(solution):
        return spread(solution)

    def keep_rows(solution):
        return lax.dynamic_slice_in_dim(solution, column * width_rows, width_rows, 1)

    def blocks(array, pair):
        return array[0, pair, :, 0, :, 0]

    def pattern(kind, pair):
        return block_pattern[0, kind, pair, :, 0, :, 0]

    fore_zero = solve(None, right_sides[0], lower_list[0], False)
    copy_zero = copy_out(fore_zero)
    into_one = couple(blocks(lower_sub, 0), pattern(0, 0), copy_zero)
    into_two = couple(blocks(lower_sub, 1), pattern(0, 1), copy_zero)
    into_top = couple(blocks(lower_top, 0), pattern(1, 0), copy_zero)
    fore_one = solve(into_one, right_sides[1], lower_list[1], False)
    copy_one = copy_out(fore_one)
    into_two = into_two + couple(blocks(lower_sub, 2), pattern(0, 2), copy_one)
    into_top = into_top + couple(blocks(lower_top, 1), pattern(1, 1), copy_one)
    fore_two = solve(into_two, right_sides[2], lower_list[2], False)
    copy_two = copy_out(fore_two)
    into_top = into_top + couple(blocks(lower_top, 2), pattern(1, 2), copy_two)
    fore_top = solve(into_top, right_sides[3], lower_list[3], True)
    final_top = solve(None, fore_top, upper_list[3], False)
    down_top = copy_out(final_top)
    toward_two = couple(blocks(upper_top, 2), pattern(3, 2), down_top)
    toward_one = couple(blocks(upper_top, 1), pattern(3, 1), down_top)
    toward_zero = couple(blocks(upper_top, 0), pattern(3, 0), down_top)
    final_two = solve(toward_two, fore_two, upper_list[2], False)
    down_two = copy_out(final_two)
    toward_one = toward_one + couple(blocks(upper_sub, 2), pattern(2, 2), down_two)
    toward_zero = toward_zero + couple(blocks(upper_sub, 1), pattern(2, 1), down_two)
    final_one = solve(toward_one, fore_one, upper_list[1], False)
    down_one = copy_out(final_one)
    toward_zero = toward_zero + couple(blocks(upper_sub, 0), pattern(2, 0), down_one)
    final_zero = solve(toward_zero, fore_zero, upper_list[0], False)
    solution_sub = jnp.stack([keep_rows(final_zero), keep_rows(final_one), keep_rows(final_two)])[
        None, :, :, None
    ]
    solution_top = keep_rows(final_top)[:, None]
    return (solution_sub, solution_top)


def solution(mesh):
    placed = (
        P("layer", None, None, "row", "col", None),
        P(None, "row", "col", None),
        P("layer", None, None, "row", "col", None),
        P(None, "row", "col", None),
        P("layer", None, None, "row", "col", None),
        P(None, "row", "col", None),
        P("layer", None, None, "row", None, "col", None, None),
        P("layer", None, None, "row", None, "col", None, None),
        P("layer", None, None, "row", None, "col", None, None),
        P("layer", None, None, "row", None, "col", None, None),
        P("layer", None, None, None, "row", None, "col"),
    )
    layers, grid = mesh.shape["layer"], mesh.shape["row"]

    def choose(*arguments):
        rhs_sub, rhs_top, inverse = arguments[0], arguments[1], arguments[3]
        columns, width = rhs_top.shape[-1] // grid, inverse.shape[-1]
        square = mesh.shape["row"] == mesh.shape["col"] and rhs_sub.shape[2] == 1
        held = 4 * 4 * LEVELS * grid * width * width
        if square and grid == 4 and rhs_top.shape[-1] % (128 * grid) == 0 and held <= 2**24:
            return solve_in_kernel(layers, grid, *arguments)
        return on_device(*arguments)

    return jax.shard_map(
        choose,
        mesh=mesh,
        in_specs=placed,
        out_specs=(P("layer", None, None, "row", "col", None), P(None, "row", "col", None)),
        check_vma=False,
    )
```

```python
import functools
import jax
import jax.numpy as jnp
from jax import lax
from jax.experimental import pallas as pl
from jax.experimental.pallas import tpu as pltpu
from jax.sharding import PartitionSpec as P

HIGHEST = lax.Precision.HIGHEST
MESH = pl.DeviceIdType.MESH
LEVELS = 3


def halves(value):
    high = value.astype(jnp.bfloat16)
    return high, (value - high.astype(jnp.float32)).astype(jnp.bfloat16)


def pair(value):
    return jnp.concatenate(halves(value), axis=1)


def dot(a, paired):
    high, low = halves(a)
    both = jnp.dot(high, paired, preferred_element_type=jnp.float32)
    both = both + jnp.dot(low, paired, preferred_element_type=jnp.float32)
    columns = paired.shape[1] // 2
    return both[:, :columns] + both[:, columns:]


def kernel(
    layers,
    grid,
    pattern,
    rhs_sub,
    rhs_top,
    lower_inv_sub,
    lower_inv_top,
    upper_inv_sub,
    upper_inv_top,
    lower_sub,
    lower_top,
    upper_sub,
    upper_top,
    out_sub,
    out_top,
    own,
    own_rhs,
    coupling,
    rhs_split,
    rhs_stage,
    rhs_full,
    inv_stage,
    inv_full,
    part,
    given,
    arrived,
    solved,
    cross,
    out_stage,
    out_full,
    own_sem,
    own_rhs_sem,
    own_inv_sem,
    coupling_sem,
    rhs_sem,
    rhs_z_sem,
    inv_sem,
    inv_z_sem,
    share_sem,
    part_sem,
    cross_sem,
    out_z_sem,
    out_sem,
):
    layer, row, col = lax.axis_index("layer"), lax.axis_index("row"), lax.axis_index("col")
    width = part.shape[2]
    columns = part.shape[3]
    others = range(1, grid)

    def ahead(me, step, count=grid):
        return lax.rem(me + step, count)

    barrier = pltpu.get_barrier_semaphore()
    for step in others:
        pl.semaphore_signal(barrier, inc=1, device_id=(layer, ahead(row, step), col), device_id_type=MESH)
        pl.semaphore_signal(barrier, inc=1, device_id=(layer, row, ahead(col, step)), device_id_type=MESH)
    for step in range(1, layers):
        pl.semaphore_signal(
            barrier, inc=1, device_id=(ahead(layer, step, layers), row, col), device_id_type=MESH
        )

    def remote(source, target, sems, index, step, device):
        return pltpu.make_async_remote_copy(
            src_ref=source,
            dst_ref=target,
            send_sem=sems.at[0, index, step - 1],
            recv_sem=sems.at[1, index, step - 1],
            device_id=device,
            device_id_type=MESH,
        )

    sources = (
        (lower_sub, 0, 0),
        (lower_sub, 1, 0),
        (lower_sub, 2, 0),
        (lower_top, 0, 1),
        (lower_top, 1, 1),
        (lower_top, 2, 1),
        (upper_top, 2, 3),
        (upper_top, 1, 3),
        (upper_sub, 2, 2),
        (upper_top, 0, 3),
        (upper_sub, 1, 2),
        (upper_sub, 0, 2),
    )
    inverses = tuple(lower_inv_sub.at[k] for k in range(LEVELS)) + (lower_inv_top,)
    inverses += tuple(upper_inv_sub.at[k] for k in range(LEVELS)) + (upper_inv_top,)
    rights = tuple(rhs_sub.at[k] for k in range(LEVELS)) + (rhs_top,)

    def own_copy(k):
        ref, at, _ = sources[k]
        return pltpu.make_async_copy(ref.at[at], own.at[k], own_sem.at[k])

    def own_rhs_copy(k):
        return pltpu.make_async_copy(rights[k], own_rhs.at[k], own_rhs_sem.at[k])

    def own_inv_copy(k):
        return pltpu.make_async_copy(inverses[k], inv_stage.at[k, row], own_inv_sem.at[k])

    own_rhs_copy(0).start()
    own_inv_copy(0).start()
    own_copy(0).start()
    for k in range(1, LEVELS + 1):
        own_rhs_copy(k).start()
        own_inv_copy(k).start()
    for k in range(1, len(sources)):
        own_copy(k).start()
    for k in range(LEVELS + 1, len(inverses)):
        own_inv_copy(k).start()

    def mask(k):
        _, at, kind = sources[k]
        own_copy(k).wait()
        coupling[k, row] = own[k] * pattern[kind * LEVELS + at].astype(jnp.float32)

    half = grid // 2
    beside = row + 1 - 2 * lax.rem(row, 2)
    above = lax.rem(row + half, grid)
    upper, lower = pl.ds(0, width // 2), pl.ds(width // 2, width // 2)

    def coupling_copy(k, step):
        to = (beside, above)[step - 1]
        return remote(coupling.at[k, row], coupling.at[k, row], coupling_sem, k, step, (layer, to, col))

    def relay_copy(k, step):
        come, to, part_rows = ((beside, above, upper), (above, beside, lower))[step - 1]
        block = coupling.at[k, come, part_rows]
        return remote(block, block, coupling_sem, k, step + 2, (layer, to, col))

    def relay(k):
        for step in (1, 2):
            coupling_copy(k, step).wait_recv()
            copy = relay_copy(k, step)
            copy.start()
            sent.append(copy)

    def rhs_copy(k, step):
        to = ahead(row, step)
        return remote(rhs_split.at[k, to], rhs_stage.at[k, row], rhs_sem, k, step, (layer, to, col))

    rows = width // grid
    share = rows // layers

    def inv_rows(k):
        return (layer * share, share) if k % (LEVELS + 1) == LEVELS else (0, rows)

    def inv_copy(k, step):
        to = (beside, above)[step - 1]
        block = inv_stage.at[k, row, pl.ds(*inv_rows(k))]
        return remote(block, block, inv_sem, k, step, (layer, to, col))

    def inv_relay_copy(k, step):
        come, to, second = ((beside, above, 0), (above, beside, 1))[step - 1]
        first, count = inv_rows(k)
        block = inv_stage.at[k, come, pl.ds(first + second * (count // 2), count // 2)]
        return remote(block, block, inv_sem, k, step + 2, (layer, to, col))

    def rhs_z_copy(k, step):
        to = ahead(col, step)
        return remote(rhs_stage.at[k, to], rhs_full.at[k, col], rhs_z_sem, k, step, (layer, row, to))

    def inv_z_copy(k, step):
        to = ahead(col, step)
        at = pl.ds(*inv_rows(k))
        return remote(inv_stage.at[k, to, at], inv_full.at[k, col, at], inv_z_sem, k, step, (layer, row, to))

    def inv_share_copy(k, step):
        block = inv_full.at[k, :, pl.ds(*inv_rows(k))]
        to = ahead(layer, step, layers)
        return remote(block, block, share_sem, k // (LEVELS + 1), step, (to, row, col))

    mate = col + 1 - 2 * lax.rem(col, 2)
    keep, give = lax.rem(col + half, grid), lax.rem(mate + half, grid)

    def give_copy(k):
        return remote(part.at[k, give], given.at[k], part_sem, k, 1, (layer, row, mate))

    def near_copy(k):
        return remote(part.at[k, mate], arrived.at[k, 0], part_sem, k, 2, (layer, row, mate))

    def far_copy(k):
        return remote(part.at[k, keep], arrived.at[k, 1], part_sem, k, 3, (layer, row, keep))

    def cross_copy(step):
        return remote(
            cross.at[0], cross.at[step], cross_sem, 0, step, (ahead(layer, step, layers), row, col)
        )

    def out_z_copy(k, step):
        to = ahead(col, step)
        return remote(solved.at[k, to], out_stage.at[k, col], out_z_sem, k, step, (layer, row, to))

    def out_copy(k, step):
        to = ahead(row, step)
        return remote(out_stage.at[k, to], out_full.at[k, row], out_sem, k, step, (layer, to, col))

    sent = []

    def start(make, k):
        for step in others:
            copy = make(k, step)
            copy.start()
            sent.append(copy)

    def arrive(make, k):
        for step in others:
            make(k, step).wait_recv()

    def spread_coupling(k):
        mask(k)
        for step in (1, 2):
            copy = coupling_copy(k, step)
            copy.start()
            sent.append(copy)

    def rhs_row(k):
        start(rhs_copy, k)
        rhs_stage[k, row] = rhs_split[k, row]

    def inv_row(k):
        own_inv_copy(k).wait()
        for step in (1, 2):
            copy = inv_copy(k, step)
            copy.start()
            sent.append(copy)

    def inv_relay(k):
        for step in (1, 2):
            inv_copy(k, step).wait_recv()
            copy = inv_relay_copy(k, step)
            copy.start()
            sent.append(copy)

    def rhs_col(k):
        arrive(rhs_copy, k)
        start(rhs_z_copy, k)
        rhs_full[k, col] = rhs_stage[k, col]

    def inv_col(k):
        for step in (1, 2):
            inv_relay_copy(k, step).wait_recv()
        start(inv_z_copy, k)
        at = pl.ds(*inv_rows(k))
        inv_full[k, col, at] = inv_stage[k, col, at]

    def inv_share(k):
        arrive(inv_z_copy, k)
        for step in range(1, layers):
            copy = inv_share_copy(k, step)
            copy.start()
            sent.append(copy)

    def split(k):
        own_rhs_copy(k).wait()
        for piece in range(grid):
            rhs_split[k, piece] = own_rhs[k, :, piece * columns : (piece + 1) * columns]

    def right_side(k):
        arrive(rhs_z_copy, k)
        return rhs_full[k].reshape(width, columns)

    def apply_inverse(k, value):
        if k % (LEVELS + 1) == LEVELS:
            for step in range(1, layers):
                inv_share_copy(k, step).wait_recv()
        else:
            arrive(inv_z_copy, k)
        return dot(inv_full[k].reshape(width, width), pair(value))

    def couple(level, k, value, first, send):
        for step in (1, 2):
            relay_copy(k, step).wait_recv()

        def add(to):
            product = dot(coupling[k, to], value)
            if not first:
                product = part[level, to] + product
            part[level, to] = product

        if not send:

            def body(to, carry):
                add(to)
                return carry

            lax.fori_loop(0, grid, body, 0)
            return

        add(give)
        give_copy(level).start()
        add(mate)
        near_copy(level).start()
        add(keep)
        give_copy(level).wait_recv()
        part[level, keep] = part[level, keep] + given[level]
        far_copy(level).start()
        add(col)
        sent.extend((give_copy(level), near_copy(level), far_copy(level)))

    def reduced(level):
        near_copy(level).wait_recv()
        total = part[level, col] + arrived[level, 0]
        far_copy(level).wait_recv()
        return total + arrived[level, 1]

    def emit(k, value):
        solved[k] = value.reshape(grid, rows, columns)
        start(out_z_copy, k)
        out_stage[k, col] = solved[k, col]

    def emit_row(k):
        arrive(out_z_copy, k)
        start(out_copy, k)
        out_full[k, row] = out_stage[k, row]

    pl.semaphore_wait(barrier, 2 * (grid - 1) + layers - 1)
    split(0)
    rhs_row(0)
    inv_row(0)
    spread_coupling(0)
    for k in range(1, LEVELS + 1):
        split(k)
    rhs_row(1)
    inv_row(1)
    inv_relay(0)
    spread_coupling(1)
    rhs_col(0)
    inv_col(0)
    spread_coupling(2)
    inv_relay(1)
    relay(0)
    rhs_col(1)
    inv_col(1)
    rhs_row(2)
    inv_row(2)
    spread_coupling(3)
    fore_zero = apply_inverse(0, right_side(0))
    fore_zero_pair = pair(fore_zero)
    couple(0, 0, fore_zero_pair, True, True)
    relay(1)
    inv_relay(2)
    spread_coupling(4)
    relay(2)
    spread_coupling(5)
    rhs_row(3)
    inv_row(3)
    couple(1, 1, fore_zero_pair, True, False)
    total = reduced(0)
    rhs_col(2)
    inv_col(2)
    fore_one = apply_inverse(1, right_side(1) - total)
    fore_one_pair = pair(fore_one)
    couple(1, 2, fore_one_pair, False, True)
    relay(3)
    spread_coupling(6)
    inv_row(7)
    inv_row(6)
    relay(4)
    spread_coupling(7)
    inv_relay(3)
    couple(2, 3, fore_zero_pair, True, False)
    rhs_col(3)
    inv_col(3)
    couple(2, 4, fore_one_pair, False, False)
    total = reduced(1)
    inv_relay(7)
    inv_relay(6)
    relay(5)
    fore_two = apply_inverse(2, right_side(2) - total)
    spread_coupling(8)
    couple(2, 5, pair(fore_two), False, True)
    relay(6)
    spread_coupling(9)
    inv_row(5)
    inv_row(4)
    inv_col(7)
    inv_col(6)
    relay(7)
    inv_relay(5)
    inv_relay(4)
    spread_coupling(10)
    inv_share(3)
    inv_share(7)
    rhs_last = right_side(3)
    cross[0] = reduced(2)
    for step in range(1, layers):
        cross_copy(step).start()
    total = cross[0]
    for step in range(1, layers):
        cross_copy(step).wait_recv()
        total = total + cross[step]
    final_top = apply_inverse(7, apply_inverse(3, rhs_last - total))
    final_top_pair = pair(final_top)
    couple(3, 6, final_top_pair, True, True)
    emit(3, final_top)
    relay(8)
    spread_coupling(11)
    couple(4, 7, final_top_pair, True, False)
    relay(9)
    residual = fore_two - reduced(3)
    inv_col(5)
    final_two = apply_inverse(6, residual)
    final_two_pair = pair(final_two)
    couple(4, 8, final_two_pair, False, True)
    emit(2, final_two)
    emit_row(3)
    relay(10)
    couple(5, 9, final_top_pair, True, False)
    relay(11)
    couple(5, 10, final_two_pair, False, False)
    residual = fore_one - reduced(4)
    inv_col(4)
    final_one = apply_inverse(5, residual)
    couple(5, 11, pair(final_one), False, True)
    emit(1, final_one)
    emit_row(2)
    final_zero = apply_inverse(4, fore_zero - reduced(5))
    emit(0, final_zero)
    emit_row(1)
    emit_row(0)

    for k in (3, 2, 1, 0):
        arrive(out_copy, k)
        for piece in range(grid):
            target = out_top if k == LEVELS else out_sub.at[k]
            target[:, piece * columns : (piece + 1) * columns] = out_full[k, piece]
    for copy in sent:
        copy.wait_send()
    for step in range(1, layers):
        cross_copy(step).wait_send()


def solve_in_kernel(
    layers,
    grid,
    rhs_sub,
    rhs_top,
    lower_inv_sub,
    lower_inv_top,
    upper_inv_sub,
    upper_inv_top,
    lower_sub,
    lower_top,
    upper_sub,
    upper_top,
    block_pattern,
):
    rows, count = rhs_top.shape[-2:]
    width = lower_inv_top.shape[-1]
    columns = count // grid
    levels = LEVELS + 1
    steps = 2 * LEVELS
    couplings = 4 * LEVELS
    f32 = jnp.float32

    def sub(array):
        return array.reshape((LEVELS,) + array.shape[-2:])

    def top(array):
        return array.reshape(array.shape[-2:])

    def sems(number, peers=grid):
        return pltpu.SemaphoreType.DMA((2, number, peers - 1))

    vmem = pl.BlockSpec(memory_space=pltpu.VMEM)
    out_sub, out_top = pl.pallas_call(
        functools.partial(kernel, layers, grid),
        out_shape=(
            jax.ShapeDtypeStruct((LEVELS, rows, count), f32),
            jax.ShapeDtypeStruct((rows, count), f32),
        ),
        in_specs=[pl.BlockSpec(memory_space=pltpu.SMEM)] + [pl.BlockSpec(memory_space=pltpu.HBM)] * 10,
        out_specs=(vmem, vmem),
        scratch_shapes=[
            pltpu.VMEM((couplings, width, width), f32),
            pltpu.VMEM((levels, rows, count), f32),
            pltpu.VMEM((couplings, grid, width, width), f32),
            pltpu.VMEM((levels, grid, rows, columns), f32),
            pltpu.VMEM((levels, grid, rows, columns), f32),
            pltpu.VMEM((levels, grid, rows, columns), f32),
            pltpu.VMEM((2 * levels, grid, rows, width), f32),
            pltpu.VMEM((2 * levels, grid, rows, width), f32),
            pltpu.VMEM((steps, grid, width, columns), f32),
            pltpu.VMEM((steps, width, columns), f32),
            pltpu.VMEM((steps, 2, width, columns), f32),
            pltpu.VMEM((levels, grid, rows, columns), f32),
            pltpu.VMEM((layers, width, columns), f32),
            pltpu.VMEM((levels, grid, rows, columns), f32),
            pltpu.VMEM((levels, grid, rows, columns), f32),
            pltpu.SemaphoreType.DMA((couplings,)),
            pltpu.SemaphoreType.DMA((levels,)),
            pltpu.SemaphoreType.DMA((2 * levels,)),
            pltpu.SemaphoreType.DMA((2, couplings, 4)),
            sems(levels),
            sems(levels),
            pltpu.SemaphoreType.DMA((2, 2 * levels, 4)),
            sems(2 * levels),
            sems(2, layers),
            sems(steps),
            sems(1, layers),
            sems(levels),
            sems(levels),
        ],
        compiler_params=pltpu.CompilerParams(
            collective_id=0, has_side_effects=True, vmem_limit_bytes=60 * 2**20
        ),
        cost_estimate=pl.CostEstimate(
            flops=2 * couplings * grid * width * width * columns,
            bytes_accessed=4 * couplings * width * width,
            transcendentals=0,
        ),
    )(
        block_pattern.reshape(-1),
        sub(rhs_sub),
        top(rhs_top),
        sub(lower_inv_sub),
        top(lower_inv_top),
        sub(upper_inv_sub),
        top(upper_inv_top),
        sub(lower_sub),
        sub(lower_top),
        sub(upper_sub),
        sub(upper_top),
    )
    return out_sub.reshape(rhs_sub.shape), out_top.reshape(rhs_top.shape)


def broadcast(x, axis, root):
    mine = lax.axis_index(axis) == root
    return lax.psum(jnp.where(mine, x, jnp.zeros_like(x)), axis)


def couple(blocks, pattern, solution):
    weighted = solution[None] * pattern[:, :, None, None].astype(jnp.float32)
    return jnp.einsum("tsab,tsbn->tan", blocks, weighted, precision=HIGHEST)


def spread(whole_block):
    return broadcast(whole_block, "row", lax.axis_index("col"))


def on_device(
    rhs_sub,
    rhs_top,
    lower_inv_sub,
    lower_inv_top,
    upper_inv_sub,
    upper_inv_top,
    lower_sub,
    lower_top,
    upper_sub,
    upper_top,
    block_pattern,
):
    column = lax.axis_index("col")
    width_rows = rhs_top.shape[2]
    gathered = (
        lax.all_gather(lower_inv_sub, "col", axis=4, tiled=True),
        lax.all_gather(lower_inv_top, "col", axis=2, tiled=True),
        lax.all_gather(upper_inv_sub, "col", axis=4, tiled=True),
        lax.all_gather(upper_inv_top, "col", axis=2, tiled=True),
        lax.all_gather(rhs_sub, "col", axis=4, tiled=True),
        lax.all_gather(rhs_top, "col", axis=2, tiled=True),
    )
    lower_list = [gathered[0][0, level, :, 0] for level in range(3)] + [gathered[1][:, 0]]
    upper_list = [gathered[2][0, level, :, 0] for level in range(3)] + [gathered[3][:, 0]]
    right_sides = [gathered[4][0, level, :, 0] for level in range(3)] + [gathered[5][:, 0]]

    def solve(partial_value, right_side, inverse_full, top):
        if partial_value is None:
            residual = right_side
        elif top:
            residual = right_side - lax.psum(partial_value, ("layer", "col"))
        else:
            residual = right_side - lax.psum(partial_value, "col")
        return jnp.einsum("kab,kbn->kan", inverse_full, residual, precision=HIGHEST)

    def copy_out(solution):
        return spread(solution)

    def keep_rows(solution):
        return lax.dynamic_slice_in_dim(solution, column * width_rows, width_rows, 1)

    def blocks(array, pair):
        return array[0, pair, :, 0, :, 0]

    def pattern(kind, pair):
        return block_pattern[0, kind, pair, :, 0, :, 0]

    fore_zero = solve(None, right_sides[0], lower_list[0], False)
    copy_zero = copy_out(fore_zero)
    into_one = couple(blocks(lower_sub, 0), pattern(0, 0), copy_zero)
    into_two = couple(blocks(lower_sub, 1), pattern(0, 1), copy_zero)
    into_top = couple(blocks(lower_top, 0), pattern(1, 0), copy_zero)
    fore_one = solve(into_one, right_sides[1], lower_list[1], False)
    copy_one = copy_out(fore_one)
    into_two = into_two + couple(blocks(lower_sub, 2), pattern(0, 2), copy_one)
    into_top = into_top + couple(blocks(lower_top, 1), pattern(1, 1), copy_one)
    fore_two = solve(into_two, right_sides[2], lower_list[2], False)
    copy_two = copy_out(fore_two)
    into_top = into_top + couple(blocks(lower_top, 2), pattern(1, 2), copy_two)
    fore_top = solve(into_top, right_sides[3], lower_list[3], True)
    final_top = solve(None, fore_top, upper_list[3], False)
    down_top = copy_out(final_top)
    toward_two = couple(blocks(upper_top, 2), pattern(3, 2), down_top)
    toward_one = couple(blocks(upper_top, 1), pattern(3, 1), down_top)
    toward_zero = couple(blocks(upper_top, 0), pattern(3, 0), down_top)
    final_two = solve(toward_two, fore_two, upper_list[2], False)
    down_two = copy_out(final_two)
    toward_one = toward_one + couple(blocks(upper_sub, 2), pattern(2, 2), down_two)
    toward_zero = toward_zero + couple(blocks(upper_sub, 1), pattern(2, 1), down_two)
    final_one = solve(toward_one, fore_one, upper_list[1], False)
    down_one = copy_out(final_one)
    toward_zero = toward_zero + couple(blocks(upper_sub, 0), pattern(2, 0), down_one)
    final_zero = solve(toward_zero, fore_zero, upper_list[0], False)
    solution_sub = jnp.stack([keep_rows(final_zero), keep_rows(final_one), keep_rows(final_two)])[
        None, :, :, None
    ]
    solution_top = keep_rows(final_top)[:, None]
    return (solution_sub, solution_top)


def solution(mesh):
    placed = (
        P("layer", None, None, "row", "col", None),
        P(None, "row", "col", None),
        P("layer", None, None, "row", "col", None),
        P(None, "row", "col", None),
        P("layer", None, None, "row", "col", None),
        P(None, "row", "col", None),
        P("layer", None, None, "row", None, "col", None, None),
        P("layer", None, None, "row", None, "col", None, None),
        P("layer", None, None, "row", None, "col", None, None),
        P("layer", None, None, "row", None, "col", None, None),
        P("layer", None, None, None, "row", None, "col"),
    )
    layers, grid = mesh.shape["layer"], mesh.shape["row"]

    def choose(*arguments):
        rhs_sub, rhs_top, inverse = arguments[0], arguments[1], arguments[3]
        columns, width = rhs_top.shape[-1] // grid, inverse.shape[-1]
        square = mesh.shape["row"] == mesh.shape["col"] and rhs_sub.shape[2] == 1
        held = 4 * 4 * LEVELS * grid * width * width
        if square and grid == 4 and rhs_top.shape[-1] % (128 * grid) == 0 and held <= 2**24:
            return solve_in_kernel(layers, grid, *arguments)
        return on_device(*arguments)

    return jax.shard_map(
        choose,
        mesh=mesh,
        in_specs=placed,
        out_specs=(P("layer", None, None, "row", "col", None), P(None, "row", "col", None)),
        check_vma=False,
    )
```

```python
import functools
import jax
import jax.numpy as jnp
from jax import lax
from jax.experimental import pallas as pl
from jax.experimental.pallas import tpu as pltpu
from jax.sharding import PartitionSpec as P

HIGHEST = lax.Precision.HIGHEST
MESH = pl.DeviceIdType.MESH
LEVELS = 3


def halves(value):
    high = value.astype(jnp.bfloat16)
    return high, (value - high.astype(jnp.float32)).astype(jnp.bfloat16)


def pair(value):
    return jnp.concatenate(halves(value), axis=1)


def dot(a, paired):
    high, low = halves(a)
    both = jnp.dot(
        jnp.concatenate((high, low), axis=0), paired, preferred_element_type=jnp.float32
    )
    both = both[: a.shape[0]] + both[a.shape[0] :]
    columns = paired.shape[1] // 2
    return both[:, :columns] + both[:, columns:]


def kernel(
    layers,
    grid,
    pattern,
    rhs_sub,
    rhs_top,
    lower_inv_sub,
    lower_inv_top,
    upper_inv_sub,
    upper_inv_top,
    lower_sub,
    lower_top,
    upper_sub,
    upper_top,
    out_sub,
    out_top,
    own,
    own_rhs,
    coupling,
    rhs_split,
    rhs_stage,
    rhs_full,
    inv_stage,
    inv_full,
    part,
    given,
    arrived,
    solved,
    cross,
    out_stage,
    out_full,
    own_sem,
    own_rhs_sem,
    own_inv_sem,
    coupling_sem,
    rhs_sem,
    rhs_z_sem,
    inv_sem,
    inv_z_sem,
    share_sem,
    part_sem,
    cross_sem,
    out_z_sem,
    out_sem,
):
    layer, row, col = lax.axis_index("layer"), lax.axis_index("row"), lax.axis_index("col")
    width = part.shape[2]
    columns = part.shape[3]
    others = range(1, grid)

    def ahead(me, step, count=grid):
        return lax.rem(me + step, count)

    barrier = pltpu.get_barrier_semaphore()
    for step in others:
        pl.semaphore_signal(barrier, inc=1, device_id=(layer, ahead(row, step), col), device_id_type=MESH)
        pl.semaphore_signal(barrier, inc=1, device_id=(layer, row, ahead(col, step)), device_id_type=MESH)
    for step in range(1, layers):
        pl.semaphore_signal(
            barrier, inc=1, device_id=(ahead(layer, step, layers), row, col), device_id_type=MESH
        )

    def remote(source, target, sems, index, step, device):
        return pltpu.make_async_remote_copy(
            src_ref=source,
            dst_ref=target,
            send_sem=sems.at[0, index, step - 1],
            recv_sem=sems.at[1, index, step - 1],
            device_id=device,
            device_id_type=MESH,
        )

    sources = (
        (lower_sub, 0, 0),
        (lower_sub, 1, 0),
        (lower_sub, 2, 0),
        (lower_top, 0, 1),
        (lower_top, 1, 1),
        (lower_top, 2, 1),
        (upper_top, 2, 3),
        (upper_top, 1, 3),
        (upper_sub, 2, 2),
        (upper_top, 0, 3),
        (upper_sub, 1, 2),
        (upper_sub, 0, 2),
    )
    inverses = tuple(lower_inv_sub.at[k] for k in range(LEVELS)) + (lower_inv_top,)
    inverses += tuple(upper_inv_sub.at[k] for k in range(LEVELS)) + (upper_inv_top,)
    rights = tuple(rhs_sub.at[k] for k in range(LEVELS)) + (rhs_top,)

    def own_copy(k):
        ref, at, _ = sources[k]
        return pltpu.make_async_copy(ref.at[at], own.at[k], own_sem.at[k])

    def own_rhs_copy(k):
        return pltpu.make_async_copy(rights[k], own_rhs.at[k], own_rhs_sem.at[k])

    def own_inv_copy(k):
        return pltpu.make_async_copy(inverses[k], inv_stage.at[k, row], own_inv_sem.at[k])

    own_rhs_copy(0).start()
    own_inv_copy(0).start()
    own_copy(0).start()
    for k in range(1, LEVELS + 1):
        own_rhs_copy(k).start()
        own_inv_copy(k).start()
    for k in range(1, len(sources)):
        own_copy(k).start()
    for k in range(LEVELS + 1, len(inverses)):
        own_inv_copy(k).start()

    def mask(k):
        _, at, kind = sources[k]
        own_copy(k).wait()
        coupling[k, row] = own[k] * pattern[kind * LEVELS + at].astype(jnp.float32)

    half = grid // 2
    beside = row + 1 - 2 * lax.rem(row, 2)
    above = lax.rem(row + half, grid)
    upper, lower = pl.ds(0, width // 2), pl.ds(width // 2, width // 2)

    def coupling_copy(k, step, second=False):
        to = (beside, above)[step - 1]
        part_rows = (upper, lower)[(step - 1) ^ second]
        block = coupling.at[k, row, part_rows]
        return remote(block, block, coupling_sem, k, step + 4 * second, (layer, to, col))

    def relay_copy(k, step):
        come, to, part_rows = ((beside, above, upper), (above, beside, lower))[step - 1]
        block = coupling.at[k, come, part_rows]
        return remote(block, block, coupling_sem, k, step + 2, (layer, to, col))

    def relay(k):
        for step in (1, 2):
            coupling_copy(k, step).wait_recv()
            copy = relay_copy(k, step)
            copy.start()
            sent.append(copy)

    def rhs_copy(k, step):
        to = ahead(row, step)
        return remote(rhs_split.at[k, to], rhs_stage.at[k, row], rhs_sem, k, step, (layer, to, col))

    rows = width // grid
    share = rows // layers

    def inv_rows(k):
        return (layer * share, share) if k % (LEVELS + 1) == LEVELS else (0, rows)

    def inv_copy(k, step):
        to = (beside, above)[step - 1]
        block = inv_stage.at[k, row, pl.ds(*inv_rows(k))]
        return remote(block, block, inv_sem, k, step, (layer, to, col))

    def inv_relay_copy(k, step):
        come, to, second = ((beside, above, 0), (above, beside, 1))[step - 1]
        first, count = inv_rows(k)
        block = inv_stage.at[k, come, pl.ds(first + second * (count // 2), count // 2)]
        return remote(block, block, inv_sem, k, step + 2, (layer, to, col))

    def rhs_z_copy(k, step):
        to = ahead(col, step)
        return remote(rhs_stage.at[k, to], rhs_full.at[k, col], rhs_z_sem, k, step, (layer, row, to))

    def inv_z_copy(k, step):
        to = ahead(col, step)
        at = pl.ds(*inv_rows(k))
        return remote(inv_stage.at[k, to, at], inv_full.at[k, col, at], inv_z_sem, k, step, (layer, row, to))

    def inv_share_copy(k, step):
        block = inv_full.at[k, :, pl.ds(*inv_rows(k))]
        to = ahead(layer, step, layers)
        return remote(block, block, share_sem, k // (LEVELS + 1), step, (to, row, col))

    mate = col + 1 - 2 * lax.rem(col, 2)
    keep, give = lax.rem(col + half, grid), lax.rem(mate + half, grid)

    def give_copy(k, at):
        rows_at = (upper, lower)[at]
        source = part.at[k, give, rows_at]
        return remote(source, given.at[k, rows_at], part_sem, k, 1 + at, (layer, row, mate))

    def near_copy(k):
        return remote(part.at[k, mate], arrived.at[k, 0], part_sem, k, 3, (layer, row, mate))

    def far_copy(k, at):
        rows_at = (upper, lower)[at]
        source = part.at[k, keep, rows_at]
        return remote(source, arrived.at[k, 1, rows_at], part_sem, k, 4 + at, (layer, row, keep))

    def cross_copy(step):
        return remote(
            cross.at[0], cross.at[step], cross_sem, 0, step, (ahead(layer, step, layers), row, col)
        )

    def out_z_copy(k, step):
        to = ahead(col, step)
        return remote(solved.at[k, to], out_stage.at[k, col], out_z_sem, k, step, (layer, row, to))

    def out_copy(k, step):
        to = ahead(row, step)
        return remote(out_stage.at[k, to], out_full.at[k, row], out_sem, k, step, (layer, to, col))

    sent = []

    def start(make, k):
        for step in others:
            copy = make(k, step)
            copy.start()
            sent.append(copy)

    def arrive(make, k):
        for step in others:
            make(k, step).wait_recv()

    def spread_masked(k):
        for second in (False, True):
            for step in (1, 2):
                copy = coupling_copy(k, step, second)
                copy.start()
                sent.append(copy)

    def spread_coupling(k):
        mask(k)
        spread_masked(k)

    def rhs_row(k):
        start(rhs_copy, k)
        rhs_stage[k, row] = rhs_split[k, row]

    def inv_row(k):
        own_inv_copy(k).wait()
        for step in (1, 2):
            copy = inv_copy(k, step)
            copy.start()
            sent.append(copy)

    def inv_relay(k):
        for step in (1, 2):
            inv_copy(k, step).wait_recv()
            copy = inv_relay_copy(k, step)
            copy.start()
            sent.append(copy)

    def rhs_col(k):
        arrive(rhs_copy, k)
        start(rhs_z_copy, k)
        rhs_full[k, col] = rhs_stage[k, col]

    def inv_col(k):
        for step in (1, 2):
            inv_relay_copy(k, step).wait_recv()
        start(inv_z_copy, k)
        at = pl.ds(*inv_rows(k))
        inv_full[k, col, at] = inv_stage[k, col, at]

    def inv_share(k):
        arrive(inv_z_copy, k)
        for step in range(1, layers):
            copy = inv_share_copy(k, step)
            copy.start()
            sent.append(copy)

    def split(k):
        own_rhs_copy(k).wait()
        for piece in range(grid):
            rhs_split[k, piece] = own_rhs[k, :, piece * columns : (piece + 1) * columns]

    def right_side(k):
        arrive(rhs_z_copy, k)
        return rhs_full[k].reshape(width, columns)

    def apply_inverse(k, value):
        if k % (LEVELS + 1) == LEVELS:
            for step in range(1, layers):
                inv_share_copy(k, step).wait_recv()
        else:
            arrive(inv_z_copy, k)
        return dot(inv_full[k].reshape(width, width), pair(value))

    def couple(level, k, value, first, send):
        for step in (1, 2):
            coupling_copy(k, step, True).wait_recv()
            relay_copy(k, step).wait_recv()

        def add(to):
            product = dot(coupling[k, to], value)
            if not first:
                product = part[level, to] + product
            part[level, to] = product

        if not send:

            def body(to, carry):
                add(to)
                return carry

            lax.fori_loop(0, grid, body, 0)
            return

        add(give)
        for at in (0, 1):
            give_copy(level, at).start()
        add(mate)
        near_copy(level).start()
        add(keep)
        for at, rows_at in ((0, upper), (1, lower)):
            give_copy(level, at).wait_recv()
            part[level, keep, rows_at] = part[level, keep, rows_at] + given[level, rows_at]
            far_copy(level, at).start()
            sent.extend((give_copy(level, at), far_copy(level, at)))
        add(col)
        sent.append(near_copy(level))

    def reduced(level):
        near_copy(level).wait_recv()
        total = part[level, col] + arrived[level, 0]
        for at in (0, 1):
            far_copy(level, at).wait_recv()
        return total + arrived[level, 1]

    def emit(k, value):
        solved[k] = value.reshape(grid, rows, columns)
        start(out_z_copy, k)
        out_stage[k, col] = solved[k, col]

    def emit_row(k):
        arrive(out_z_copy, k)
        start(out_copy, k)
        out_full[k, row] = out_stage[k, row]

    for k in range(LEVELS + 1):
        split(k)
    mask(0)
    mask(1)
    pl.semaphore_wait(barrier, 2 * (grid - 1) + layers - 1)
    rhs_row(0)
    inv_row(0)
    spread_masked(0)
    rhs_row(1)
    inv_row(1)
    inv_relay(0)
    spread_masked(1)
    rhs_col(0)
    inv_col(0)
    spread_coupling(2)
    inv_relay(1)
    relay(0)
    rhs_col(1)
    inv_col(1)
    rhs_row(2)
    inv_row(2)
    spread_coupling(3)
    fore_zero = apply_inverse(0, right_side(0))
    fore_zero_pair = pair(fore_zero)
    couple(0, 0, fore_zero_pair, True, True)
    relay(1)
    inv_relay(2)
    spread_coupling(4)
    relay(2)
    spread_coupling(5)
    rhs_row(3)
    inv_row(3)
    couple(1, 1, fore_zero_pair, True, False)
    total = reduced(0)
    rhs_col(2)
    inv_col(2)
    fore_one = apply_inverse(1, right_side(1) - total)
    fore_one_pair = pair(fore_one)
    couple(1, 2, fore_one_pair, False, True)
    relay(3)
    spread_coupling(6)
    inv_row(7)
    inv_row(6)
    relay(4)
    spread_coupling(7)
    inv_relay(3)
    couple(2, 3, fore_zero_pair, True, False)
    rhs_col(3)
    inv_col(3)
    couple(2, 4, fore_one_pair, False, False)
    total = reduced(1)
    inv_relay(7)
    inv_relay(6)
    relay(5)
    fore_two = apply_inverse(2, right_side(2) - total)
    spread_coupling(8)
    couple(2, 5, pair(fore_two), False, True)
    relay(6)
    spread_coupling(9)
    inv_row(5)
    inv_row(4)
    inv_col(7)
    inv_col(6)
    relay(7)
    inv_relay(5)
    inv_relay(4)
    spread_coupling(10)
    inv_share(3)
    inv_share(7)
    rhs_last = right_side(3)
    cross[0] = reduced(2)
    for step in range(1, layers):
        cross_copy(step).start()
    total = cross[0]
    for step in range(1, layers):
        cross_copy(step).wait_recv()
        total = total + cross[step]
    final_top = apply_inverse(7, apply_inverse(3, rhs_last - total))
    final_top_pair = pair(final_top)
    couple(3, 6, final_top_pair, True, True)
    emit(3, final_top)
    relay(8)
    spread_coupling(11)
    couple(4, 7, final_top_pair, True, False)
    relay(9)
    residual = fore_two - reduced(3)
    inv_col(5)
    final_two = apply_inverse(6, residual)
    final_two_pair = pair(final_two)
    couple(4, 8, final_two_pair, False, True)
    emit(2, final_two)
    emit_row(3)
    relay(10)
    couple(5, 9, final_top_pair, True, False)
    relay(11)
    couple(5, 10, final_two_pair, False, False)
    residual = fore_one - reduced(4)
    inv_col(4)
    final_one = apply_inverse(5, residual)
    couple(5, 11, pair(final_one), False, True)
    emit(1, final_one)
    emit_row(2)
    final_zero = apply_inverse(4, fore_zero - reduced(5))
    emit(0, final_zero)
    emit_row(1)
    emit_row(0)

    for k in (3, 2, 1, 0):
        arrive(out_copy, k)
        for piece in range(grid):
            target = out_top if k == LEVELS else out_sub.at[k]
            target[:, piece * columns : (piece + 1) * columns] = out_full[k, piece]
    for copy in sent:
        copy.wait_send()
    for step in range(1, layers):
        cross_copy(step).wait_send()


def solve_in_kernel(
    layers,
    grid,
    rhs_sub,
    rhs_top,
    lower_inv_sub,
    lower_inv_top,
    upper_inv_sub,
    upper_inv_top,
    lower_sub,
    lower_top,
    upper_sub,
    upper_top,
    block_pattern,
):
    rows, count = rhs_top.shape[-2:]
    width = lower_inv_top.shape[-1]
    columns = count // grid
    levels = LEVELS + 1
    steps = 2 * LEVELS
    couplings = 4 * LEVELS
    f32 = jnp.float32

    def sub(array):
        return array.reshape((LEVELS,) + array.shape[-2:])

    def top(array):
        return array.reshape(array.shape[-2:])

    def sems(number, peers=grid):
        return pltpu.SemaphoreType.DMA((2, number, peers - 1))

    vmem = pl.BlockSpec(memory_space=pltpu.VMEM)
    out_sub, out_top = pl.pallas_call(
        functools.partial(kernel, layers, grid),
        out_shape=(
            jax.ShapeDtypeStruct((LEVELS, rows, count), f32),
            jax.ShapeDtypeStruct((rows, count), f32),
        ),
        in_specs=[pl.BlockSpec(memory_space=pltpu.SMEM)] + [pl.BlockSpec(memory_space=pltpu.HBM)] * 10,
        out_specs=(vmem, vmem),
        scratch_shapes=[
            pltpu.VMEM((couplings, width, width), f32),
            pltpu.VMEM((levels, rows, count), f32),
            pltpu.VMEM((couplings, grid, width, width), f32),
            pltpu.VMEM((levels, grid, rows, columns), f32),
            pltpu.VMEM((levels, grid, rows, columns), f32),
            pltpu.VMEM((levels, grid, rows, columns), f32),
            pltpu.VMEM((2 * levels, grid, rows, width), f32),
            pltpu.VMEM((2 * levels, grid, rows, width), f32),
            pltpu.VMEM((steps, grid, width, columns), f32),
            pltpu.VMEM((steps, width, columns), f32),
            pltpu.VMEM((steps, 2, width, columns), f32),
            pltpu.VMEM((levels, grid, rows, columns), f32),
            pltpu.VMEM((layers, width, columns), f32),
            pltpu.VMEM((levels, grid, rows, columns), f32),
            pltpu.VMEM((levels, grid, rows, columns), f32),
            pltpu.SemaphoreType.DMA((couplings,)),
            pltpu.SemaphoreType.DMA((levels,)),
            pltpu.SemaphoreType.DMA((2 * levels,)),
            pltpu.SemaphoreType.DMA((2, couplings, 6)),
            sems(levels),
            sems(levels),
            pltpu.SemaphoreType.DMA((2, 2 * levels, 4)),
            sems(2 * levels),
            sems(2, layers),
            pltpu.SemaphoreType.DMA((2, steps, 5)),
            sems(1, layers),
            sems(levels),
            sems(levels),
        ],
        compiler_params=pltpu.CompilerParams(
            collective_id=0, has_side_effects=True, vmem_limit_bytes=60 * 2**20
        ),
        cost_estimate=pl.CostEstimate(
            flops=2 * couplings * grid * width * width * columns,
            bytes_accessed=4 * couplings * width * width,
            transcendentals=0,
        ),
    )(
        block_pattern.reshape(-1),
        sub(rhs_sub),
        top(rhs_top),
        sub(lower_inv_sub),
        top(lower_inv_top),
        sub(upper_inv_sub),
        top(upper_inv_top),
        sub(lower_sub),
        sub(lower_top),
        sub(upper_sub),
        sub(upper_top),
    )
    return out_sub.reshape(rhs_sub.shape), out_top.reshape(rhs_top.shape)


def broadcast(x, axis, root):
    mine = lax.axis_index(axis) == root
    return lax.psum(jnp.where(mine, x, jnp.zeros_like(x)), axis)


def couple(blocks, pattern, solution):
    weighted = solution[None] * pattern[:, :, None, None].astype(jnp.float32)
    return jnp.einsum("tsab,tsbn->tan", blocks, weighted, precision=HIGHEST)


def spread(whole_block):
    return broadcast(whole_block, "row", lax.axis_index("col"))


def on_device(
    rhs_sub,
    rhs_top,
    lower_inv_sub,
    lower_inv_top,
    upper_inv_sub,
    upper_inv_top,
    lower_sub,
    lower_top,
    upper_sub,
    upper_top,
    block_pattern,
):
    column = lax.axis_index("col")
    width_rows = rhs_top.shape[2]
    gathered = (
        lax.all_gather(lower_inv_sub, "col", axis=4, tiled=True),
        lax.all_gather(lower_inv_top, "col", axis=2, tiled=True),
        lax.all_gather(upper_inv_sub, "col", axis=4, tiled=True),
        lax.all_gather(upper_inv_top, "col", axis=2, tiled=True),
        lax.all_gather(rhs_sub, "col", axis=4, tiled=True),
        lax.all_gather(rhs_top, "col", axis=2, tiled=True),
    )
    lower_list = [gathered[0][0, level, :, 0] for level in range(3)] + [gathered[1][:, 0]]
    upper_list = [gathered[2][0, level, :, 0] for level in range(3)] + [gathered[3][:, 0]]
    right_sides = [gathered[4][0, level, :, 0] for level in range(3)] + [gathered[5][:, 0]]

    def solve(partial_value, right_side, inverse_full, top):
        if partial_value is None:
            residual = right_side
        elif top:
            residual = right_side - lax.psum(partial_value, ("layer", "col"))
        else:
            residual = right_side - lax.psum(partial_value, "col")
        return jnp.einsum("kab,kbn->kan", inverse_full, residual, precision=HIGHEST)

    def copy_out(solution):
        return spread(solution)

    def keep_rows(solution):
        return lax.dynamic_slice_in_dim(solution, column * width_rows, width_rows, 1)

    def blocks(array, pair):
        return array[0, pair, :, 0, :, 0]

    def pattern(kind, pair):
        return block_pattern[0, kind, pair, :, 0, :, 0]

    fore_zero = solve(None, right_sides[0], lower_list[0], False)
    copy_zero = copy_out(fore_zero)
    into_one = couple(blocks(lower_sub, 0), pattern(0, 0), copy_zero)
    into_two = couple(blocks(lower_sub, 1), pattern(0, 1), copy_zero)
    into_top = couple(blocks(lower_top, 0), pattern(1, 0), copy_zero)
    fore_one = solve(into_one, right_sides[1], lower_list[1], False)
    copy_one = copy_out(fore_one)
    into_two = into_two + couple(blocks(lower_sub, 2), pattern(0, 2), copy_one)
    into_top = into_top + couple(blocks(lower_top, 1), pattern(1, 1), copy_one)
    fore_two = solve(into_two, right_sides[2], lower_list[2], False)
    copy_two = copy_out(fore_two)
    into_top = into_top + couple(blocks(lower_top, 2), pattern(1, 2), copy_two)
    fore_top = solve(into_top, right_sides[3], lower_list[3], True)
    final_top = solve(None, fore_top, upper_list[3], False)
    down_top = copy_out(final_top)
    toward_two = couple(blocks(upper_top, 2), pattern(3, 2), down_top)
    toward_one = couple(blocks(upper_top, 1), pattern(3, 1), down_top)
    toward_zero = couple(blocks(upper_top, 0), pattern(3, 0), down_top)
    final_two = solve(toward_two, fore_two, upper_list[2], False)
    down_two = copy_out(final_two)
    toward_one = toward_one + couple(blocks(upper_sub, 2), pattern(2, 2), down_two)
    toward_zero = toward_zero + couple(blocks(upper_sub, 1), pattern(2, 1), down_two)
    final_one = solve(toward_one, fore_one, upper_list[1], False)
    down_one = copy_out(final_one)
    toward_zero = toward_zero + couple(blocks(upper_sub, 0), pattern(2, 0), down_one)
    final_zero = solve(toward_zero, fore_zero, upper_list[0], False)
    solution_sub = jnp.stack([keep_rows(final_zero), keep_rows(final_one), keep_rows(final_two)])[
        None, :, :, None
    ]
    solution_top = keep_rows(final_top)[:, None]
    return (solution_sub, solution_top)


def solution(mesh):
    placed = (
        P("layer", None, None, "row", "col", None),
        P(None, "row", "col", None),
        P("layer", None, None, "row", "col", None),
        P(None, "row", "col", None),
        P("layer", None, None, "row", "col", None),
        P(None, "row", "col", None),
        P("layer", None, None, "row", None, "col", None, None),
        P("layer", None, None, "row", None, "col", None, None),
        P("layer", None, None, "row", None, "col", None, None),
        P("layer", None, None, "row", None, "col", None, None),
        P("layer", None, None, None, "row", None, "col"),
    )
    layers, grid = mesh.shape["layer"], mesh.shape["row"]

    def choose(*arguments):
        rhs_sub, rhs_top, inverse = arguments[0], arguments[1], arguments[3]
        columns, width = rhs_top.shape[-1] // grid, inverse.shape[-1]
        square = mesh.shape["row"] == mesh.shape["col"] and rhs_sub.shape[2] == 1
        held = 4 * 4 * LEVELS * grid * width * width
        if square and grid == 4 and rhs_top.shape[-1] % (128 * grid) == 0 and held <= 2**24:
            return solve_in_kernel(layers, grid, *arguments)
        return on_device(*arguments)

    return jax.shard_map(
        choose,
        mesh=mesh,
        in_specs=placed,
        out_specs=(P("layer", None, None, "row", "col", None), P(None, "row", "col", None)),
        check_vma=False,
    )
```

```python
import functools
import jax
import jax.numpy as jnp
from jax import lax
from jax.experimental import pallas as pl
from jax.experimental.pallas import tpu as pltpu
from jax.sharding import PartitionSpec as P

HIGHEST = lax.Precision.HIGHEST
MESH = pl.DeviceIdType.MESH
LEVELS = 3


def halves(value):
    high = value.astype(jnp.bfloat16)
    return high, (value - high.astype(jnp.float32)).astype(jnp.bfloat16)


def pair(value):
    return jnp.concatenate(halves(value), axis=1)


def dot(a, paired):
    high, low = halves(a)
    both = jnp.dot(high, paired, preferred_element_type=jnp.float32)
    both = both + jnp.dot(low, paired, preferred_element_type=jnp.float32)
    columns = paired.shape[1] // 2
    return both[:, :columns] + both[:, columns:]


def kernel(
    layers,
    grid,
    pattern,
    rhs_sub,
    rhs_top,
    lower_inv_sub,
    lower_inv_top,
    upper_inv_sub,
    upper_inv_top,
    lower_sub,
    lower_top,
    upper_sub,
    upper_top,
    out_sub,
    out_top,
    own,
    own_rhs,
    coupling,
    rhs_split,
    rhs_stage,
    rhs_full,
    inv_stage,
    inv_full,
    part,
    given,
    arrived,
    solved,
    cross,
    out_stage,
    out_full,
    own_sem,
    own_rhs_sem,
    own_inv_sem,
    coupling_sem,
    rhs_sem,
    rhs_z_sem,
    inv_sem,
    inv_z_sem,
    share_sem,
    part_sem,
    cross_sem,
    out_z_sem,
    out_sem,
):
    layer, row, col = lax.axis_index("layer"), lax.axis_index("row"), lax.axis_index("col")
    width = part.shape[2]
    columns = part.shape[3]
    others = range(1, grid)

    def ahead(me, step, count=grid):
        return lax.rem(me + step, count)

    barrier = pltpu.get_barrier_semaphore()
    for step in others:
        pl.semaphore_signal(barrier, inc=1, device_id=(layer, ahead(row, step), col), device_id_type=MESH)
        pl.semaphore_signal(barrier, inc=1, device_id=(layer, row, ahead(col, step)), device_id_type=MESH)
    for step in range(1, layers):
        pl.semaphore_signal(
            barrier, inc=1, device_id=(ahead(layer, step, layers), row, col), device_id_type=MESH
        )

    def remote(source, target, sems, index, step, device):
        return pltpu.make_async_remote_copy(
            src_ref=source,
            dst_ref=target,
            send_sem=sems.at[0, index, step - 1],
            recv_sem=sems.at[1, index, step - 1],
            device_id=device,
            device_id_type=MESH,
        )

    sources = (
        (lower_sub, 0, 0),
        (lower_sub, 1, 0),
        (lower_sub, 2, 0),
        (lower_top, 0, 1),
        (lower_top, 1, 1),
        (lower_top, 2, 1),
        (upper_top, 2, 3),
        (upper_top, 1, 3),
        (upper_sub, 2, 2),
        (upper_top, 0, 3),
        (upper_sub, 1, 2),
        (upper_sub, 0, 2),
    )
    inverses = tuple(lower_inv_sub.at[k] for k in range(LEVELS)) + (lower_inv_top,)
    inverses += tuple(upper_inv_sub.at[k] for k in range(LEVELS)) + (upper_inv_top,)
    rights = tuple(rhs_sub.at[k] for k in range(LEVELS)) + (rhs_top,)

    def own_copy(k):
        ref, at, _ = sources[k]
        return pltpu.make_async_copy(ref.at[at], own.at[k], own_sem.at[k])

    def own_rhs_copy(k):
        return pltpu.make_async_copy(rights[k], own_rhs.at[k], own_rhs_sem.at[k])

    def own_inv_copy(k):
        return pltpu.make_async_copy(inverses[k], inv_stage.at[k, row], own_inv_sem.at[k])

    own_rhs_copy(0).start()
    own_inv_copy(0).start()
    own_copy(0).start()
    for k in range(1, LEVELS + 1):
        own_rhs_copy(k).start()
        own_inv_copy(k).start()
    for k in range(1, len(sources)):
        own_copy(k).start()
    for k in range(LEVELS + 1, len(inverses)):
        own_inv_copy(k).start()

    def mask(k):
        _, at, kind = sources[k]
        own_copy(k).wait()
        coupling[k, row] = own[k] * pattern[kind * LEVELS + at].astype(jnp.float32)

    half = grid // 2
    beside = row + 1 - 2 * lax.rem(row, 2)
    above = lax.rem(row + half, grid)
    upper, lower = pl.ds(0, width // 2), pl.ds(width // 2, width // 2)

    def coupling_copy(k, step):
        to = (beside, above)[step - 1]
        return remote(coupling.at[k, row], coupling.at[k, row], coupling_sem, k, step, (layer, to, col))

    def relay_copy(k, step):
        come, to, part_rows = ((beside, above, upper), (above, beside, lower))[step - 1]
        block = coupling.at[k, come, part_rows]
        return remote(block, block, coupling_sem, k, step + 2, (layer, to, col))

    def relay(k):
        for step in (1, 2):
            coupling_copy(k, step).wait_recv()
            copy = relay_copy(k, step)
            copy.start()
            sent.append(copy)

    def rhs_copy(k, step):
        to = ahead(row, step)
        return remote(rhs_split.at[k, to], rhs_stage.at[k, row], rhs_sem, k, step, (layer, to, col))

    rows = width // grid
    share = rows // layers

    def inv_rows(k):
        return (layer * share, share) if k % (LEVELS + 1) == LEVELS else (0, rows)

    def inv_copy(k, step):
        to = (beside, above)[step - 1]
        block = inv_stage.at[k, row, pl.ds(*inv_rows(k))]
        return remote(block, block, inv_sem, k, step, (layer, to, col))

    def inv_relay_copy(k, step):
        come, to, second = ((beside, above, 0), (above, beside, 1))[step - 1]
        first, count = inv_rows(k)
        block = inv_stage.at[k, come, pl.ds(first + second * (count // 2), count // 2)]
        return remote(block, block, inv_sem, k, step + 2, (layer, to, col))

    def rhs_z_copy(k, step):
        to = ahead(col, step)
        return remote(rhs_stage.at[k, to], rhs_full.at[k, col], rhs_z_sem, k, step, (layer, row, to))

    def inv_z_copy(k, step):
        to = ahead(col, step)
        at = pl.ds(*inv_rows(k))
        return remote(inv_stage.at[k, to, at], inv_full.at[k, col, at], inv_z_sem, k, step, (layer, row, to))

    def inv_share_copy(k, step):
        block = inv_full.at[k, :, pl.ds(*inv_rows(k))]
        to = ahead(layer, step, layers)
        return remote(block, block, share_sem, k // (LEVELS + 1), step, (to, row, col))

    mate = col + 1 - 2 * lax.rem(col, 2)
    keep, give = lax.rem(col + half, grid), lax.rem(mate + half, grid)

    def give_copy(k):
        return remote(part.at[k, give], given.at[k], part_sem, k, 1, (layer, row, mate))

    def near_copy(k):
        return remote(part.at[k, mate], arrived.at[k, 0], part_sem, k, 2, (layer, row, mate))

    def far_copy(k):
        return remote(part.at[k, keep], arrived.at[k, 1], part_sem, k, 3, (layer, row, keep))

    def cross_copy(step):
        return remote(
            cross.at[0], cross.at[step], cross_sem, 0, step, (ahead(layer, step, layers), row, col)
        )

    def out_z_copy(k, step):
        to = ahead(col, step)
        return remote(solved.at[k, to], out_stage.at[k, col], out_z_sem, k, step, (layer, row, to))

    def out_copy(k, step):
        to = ahead(row, step)
        return remote(out_stage.at[k, to], out_full.at[k, row], out_sem, k, step, (layer, to, col))

    sent = []

    def start(make, k):
        for step in others:
            copy = make(k, step)
            copy.start()
            sent.append(copy)

    def arrive(make, k):
        for step in others:
            make(k, step).wait_recv()

    def spread_masked(k):
        for step in (1, 2):
            copy = coupling_copy(k, step)
            copy.start()
            sent.append(copy)

    def spread_coupling(k):
        mask(k)
        spread_masked(k)

    def rhs_row(k):
        start(rhs_copy, k)
        rhs_stage[k, row] = rhs_split[k, row]

    def inv_row(k):
        own_inv_copy(k).wait()
        for step in (1, 2):
            copy = inv_copy(k, step)
            copy.start()
            sent.append(copy)

    def inv_relay(k):
        for step in (1, 2):
            inv_copy(k, step).wait_recv()
            copy = inv_relay_copy(k, step)
            copy.start()
            sent.append(copy)

    def rhs_col(k):
        arrive(rhs_copy, k)
        start(rhs_z_copy, k)
        rhs_full[k, col] = rhs_stage[k, col]

    def inv_col(k):
        for step in (1, 2):
            inv_relay_copy(k, step).wait_recv()
        start(inv_z_copy, k)
        at = pl.ds(*inv_rows(k))
        inv_full[k, col, at] = inv_stage[k, col, at]

    def inv_share(k):
        arrive(inv_z_copy, k)
        for step in range(1, layers):
            copy = inv_share_copy(k, step)
            copy.start()
            sent.append(copy)

    def split(k):
        own_rhs_copy(k).wait()
        for piece in range(grid):
            rhs_split[k, piece] = own_rhs[k, :, piece * columns : (piece + 1) * columns]

    def right_side(k):
        arrive(rhs_z_copy, k)
        return rhs_full[k].reshape(width, columns)

    def apply_inverse(k, value):
        if k % (LEVELS + 1) == LEVELS:
            for step in range(1, layers):
                inv_share_copy(k, step).wait_recv()
        else:
            arrive(inv_z_copy, k)
        return dot(inv_full[k].reshape(width, width), pair(value))

    def couple(level, k, value, first, send):
        for step in (1, 2):
            relay_copy(k, step).wait_recv()

        def add(to):
            product = dot(coupling[k, to], value)
            if not first:
                product = part[level, to] + product
            part[level, to] = product

        if not send:

            def body(to, carry):
                add(to)
                return carry

            lax.fori_loop(0, grid, body, 0)
            return

        add(give)
        give_copy(level).start()
        add(mate)
        near_copy(level).start()
        add(keep)
        give_copy(level).wait_recv()
        part[level, keep] = part[level, keep] + given[level]
        far_copy(level).start()
        add(col)
        sent.extend((give_copy(level), near_copy(level), far_copy(level)))

    def reduced(level):
        near_copy(level).wait_recv()
        total = part[level, col] + arrived[level, 0]
        far_copy(level).wait_recv()
        return total + arrived[level, 1]

    def emit(k, value):
        solved[k] = value.reshape(grid, rows, columns)
        start(out_z_copy, k)
        out_stage[k, col] = solved[k, col]

    def emit_row(k):
        arrive(out_z_copy, k)
        start(out_copy, k)
        out_full[k, row] = out_stage[k, row]

    split(0)
    mask(0)
    pl.semaphore_wait(barrier, 2 * (grid - 1) + layers - 1)
    rhs_row(0)
    inv_row(0)
    spread_masked(0)
    for k in range(1, LEVELS + 1):
        split(k)
    inv_relay(0)
    rhs_col(0)
    inv_col(0)
    spread_coupling(1)
    relay(0)
    rhs_row(1)
    inv_row(1)
    spread_coupling(2)
    inv_relay(1)
    relay(1)
    rhs_row(2)
    inv_row(2)
    spread_coupling(3)
    fore_zero = apply_inverse(0, right_side(0))
    fore_zero_pair = pair(fore_zero)
    couple(0, 0, fore_zero_pair, True, True)
    rhs_col(1)
    inv_col(1)
    inv_relay(2)
    spread_coupling(4)
    relay(2)
    spread_coupling(5)
    couple(1, 1, fore_zero_pair, True, False)
    relay(3)
    rhs_row(3)
    inv_row(3)
    total = reduced(0)
    rhs_col(2)
    inv_col(2)
    fore_one = apply_inverse(1, right_side(1) - total)
    fore_one_pair = pair(fore_one)
    couple(1, 2, fore_one_pair, False, True)
    relay(4)
    spread_coupling(6)
    inv_relay(3)
    relay(5)
    inv_row(7)
    inv_row(6)
    spread_coupling(7)
    couple(2, 3, fore_zero_pair, True, False)
    rhs_col(3)
    inv_col(3)
    couple(2, 4, fore_one_pair, False, False)
    total = reduced(1)
    inv_relay(7)
    inv_relay(6)
    fore_two = apply_inverse(2, right_side(2) - total)
    spread_coupling(8)
    couple(2, 5, pair(fore_two), False, True)
    relay(6)
    spread_coupling(9)
    inv_row(5)
    inv_row(4)
    inv_col(7)
    inv_col(6)
    relay(7)
    inv_relay(5)
    inv_relay(4)
    spread_coupling(10)
    inv_share(3)
    inv_share(7)
    rhs_last = right_side(3)
    cross[0] = reduced(2)
    for step in range(1, layers):
        cross_copy(step).start()
    total = cross[0]
    for step in range(1, layers):
        cross_copy(step).wait_recv()
        total = total + cross[step]
    final_top = apply_inverse(7, apply_inverse(3, rhs_last - total))
    final_top_pair = pair(final_top)
    couple(3, 6, final_top_pair, True, True)
    emit(3, final_top)
    relay(8)
    spread_coupling(11)
    couple(4, 7, final_top_pair, True, False)
    relay(9)
    residual = fore_two - reduced(3)
    inv_col(5)
    final_two = apply_inverse(6, residual)
    final_two_pair = pair(final_two)
    couple(4, 8, final_two_pair, False, True)
    emit(2, final_two)
    emit_row(3)
    relay(10)
    couple(5, 9, final_top_pair, True, False)
    relay(11)
    couple(5, 10, final_two_pair, False, False)
    residual = fore_one - reduced(4)
    inv_col(4)
    final_one = apply_inverse(5, residual)
    couple(5, 11, pair(final_one), False, True)
    emit(1, final_one)
    emit_row(2)
    final_zero = apply_inverse(4, fore_zero - reduced(5))
    emit(0, final_zero)
    emit_row(1)
    emit_row(0)

    for k in (3, 2, 1, 0):
        arrive(out_copy, k)
        for piece in range(grid):
            target = out_top if k == LEVELS else out_sub.at[k]
            target[:, piece * columns : (piece + 1) * columns] = out_full[k, piece]
    for copy in sent:
        copy.wait_send()
    for step in range(1, layers):
        cross_copy(step).wait_send()


def solve_in_kernel(
    layers,
    grid,
    rhs_sub,
    rhs_top,
    lower_inv_sub,
    lower_inv_top,
    upper_inv_sub,
    upper_inv_top,
    lower_sub,
    lower_top,
    upper_sub,
    upper_top,
    block_pattern,
):
    rows, count = rhs_top.shape[-2:]
    width = lower_inv_top.shape[-1]
    columns = count // grid
    levels = LEVELS + 1
    steps = 2 * LEVELS
    couplings = 4 * LEVELS
    f32 = jnp.float32

    def sub(array):
        return array.reshape((LEVELS,) + array.shape[-2:])

    def top(array):
        return array.reshape(array.shape[-2:])

    def sems(number, peers=grid):
        return pltpu.SemaphoreType.DMA((2, number, peers - 1))

    vmem = pl.BlockSpec(memory_space=pltpu.VMEM)
    out_sub, out_top = pl.pallas_call(
        functools.partial(kernel, layers, grid),
        out_shape=(
            jax.ShapeDtypeStruct((LEVELS, rows, count), f32),
            jax.ShapeDtypeStruct((rows, count), f32),
        ),
        in_specs=[pl.BlockSpec(memory_space=pltpu.SMEM)] + [pl.BlockSpec(memory_space=pltpu.HBM)] * 10,
        out_specs=(vmem, vmem),
        scratch_shapes=[
            pltpu.VMEM((couplings, width, width), f32),
            pltpu.VMEM((levels, rows, count), f32),
            pltpu.VMEM((couplings, grid, width, width), f32),
            pltpu.VMEM((levels, grid, rows, columns), f32),
            pltpu.VMEM((levels, grid, rows, columns), f32),
            pltpu.VMEM((levels, grid, rows, columns), f32),
            pltpu.VMEM((2 * levels, grid, rows, width), f32),
            pltpu.VMEM((2 * levels, grid, rows, width), f32),
            pltpu.VMEM((steps, grid, width, columns), f32),
            pltpu.VMEM((steps, width, columns), f32),
            pltpu.VMEM((steps, 2, width, columns), f32),
            pltpu.VMEM((levels, grid, rows, columns), f32),
            pltpu.VMEM((layers, width, columns), f32),
            pltpu.VMEM((levels, grid, rows, columns), f32),
            pltpu.VMEM((levels, grid, rows, columns), f32),
            pltpu.SemaphoreType.DMA((couplings,)),
            pltpu.SemaphoreType.DMA((levels,)),
            pltpu.SemaphoreType.DMA((2 * levels,)),
            pltpu.SemaphoreType.DMA((2, couplings, 4)),
            sems(levels),
            sems(levels),
            pltpu.SemaphoreType.DMA((2, 2 * levels, 4)),
            sems(2 * levels),
            sems(2, layers),
            sems(steps),
            sems(1, layers),
            sems(levels),
            sems(levels),
        ],
        compiler_params=pltpu.CompilerParams(
            collective_id=0, has_side_effects=True, vmem_limit_bytes=60 * 2**20
        ),
        cost_estimate=pl.CostEstimate(
            flops=2 * couplings * grid * width * width * columns,
            bytes_accessed=4 * couplings * width * width,
            transcendentals=0,
        ),
    )(
        block_pattern.reshape(-1),
        sub(rhs_sub),
        top(rhs_top),
        sub(lower_inv_sub),
        top(lower_inv_top),
        sub(upper_inv_sub),
        top(upper_inv_top),
        sub(lower_sub),
        sub(lower_top),
        sub(upper_sub),
        sub(upper_top),
    )
    return out_sub.reshape(rhs_sub.shape), out_top.reshape(rhs_top.shape)


def broadcast(x, axis, root):
    mine = lax.axis_index(axis) == root
    return lax.psum(jnp.where(mine, x, jnp.zeros_like(x)), axis)


def couple(blocks, pattern, solution):
    weighted = solution[None] * pattern[:, :, None, None].astype(jnp.float32)
    return jnp.einsum("tsab,tsbn->tan", blocks, weighted, precision=HIGHEST)


def spread(whole_block):
    return broadcast(whole_block, "row", lax.axis_index("col"))


def on_device(
    rhs_sub,
    rhs_top,
    lower_inv_sub,
    lower_inv_top,
    upper_inv_sub,
    upper_inv_top,
    lower_sub,
    lower_top,
    upper_sub,
    upper_top,
    block_pattern,
):
    column = lax.axis_index("col")
    width_rows = rhs_top.shape[2]
    gathered = (
        lax.all_gather(lower_inv_sub, "col", axis=4, tiled=True),
        lax.all_gather(lower_inv_top, "col", axis=2, tiled=True),
        lax.all_gather(upper_inv_sub, "col", axis=4, tiled=True),
        lax.all_gather(upper_inv_top, "col", axis=2, tiled=True),
        lax.all_gather(rhs_sub, "col", axis=4, tiled=True),
        lax.all_gather(rhs_top, "col", axis=2, tiled=True),
    )
    lower_list = [gathered[0][0, level, :, 0] for level in range(3)] + [gathered[1][:, 0]]
    upper_list = [gathered[2][0, level, :, 0] for level in range(3)] + [gathered[3][:, 0]]
    right_sides = [gathered[4][0, level, :, 0] for level in range(3)] + [gathered[5][:, 0]]

    def solve(partial_value, right_side, inverse_full, top):
        if partial_value is None:
            residual = right_side
        elif top:
            residual = right_side - lax.psum(partial_value, ("layer", "col"))
        else:
            residual = right_side - lax.psum(partial_value, "col")
        return jnp.einsum("kab,kbn->kan", inverse_full, residual, precision=HIGHEST)

    def copy_out(solution):
        return spread(solution)

    def keep_rows(solution):
        return lax.dynamic_slice_in_dim(solution, column * width_rows, width_rows, 1)

    def blocks(array, pair):
        return array[0, pair, :, 0, :, 0]

    def pattern(kind, pair):
        return block_pattern[0, kind, pair, :, 0, :, 0]

    fore_zero = solve(None, right_sides[0], lower_list[0], False)
    copy_zero = copy_out(fore_zero)
    into_one = couple(blocks(lower_sub, 0), pattern(0, 0), copy_zero)
    into_two = couple(blocks(lower_sub, 1), pattern(0, 1), copy_zero)
    into_top = couple(blocks(lower_top, 0), pattern(1, 0), copy_zero)
    fore_one = solve(into_one, right_sides[1], lower_list[1], False)
    copy_one = copy_out(fore_one)
    into_two = into_two + couple(blocks(lower_sub, 2), pattern(0, 2), copy_one)
    into_top = into_top + couple(blocks(lower_top, 1), pattern(1, 1), copy_one)
    fore_two = solve(into_two, right_sides[2], lower_list[2], False)
    copy_two = copy_out(fore_two)
    into_top = into_top + couple(blocks(lower_top, 2), pattern(1, 2), copy_two)
    fore_top = solve(into_top, right_sides[3], lower_list[3], True)
    final_top = solve(None, fore_top, upper_list[3], False)
    down_top = copy_out(final_top)
    toward_two = couple(blocks(upper_top, 2), pattern(3, 2), down_top)
    toward_one = couple(blocks(upper_top, 1), pattern(3, 1), down_top)
    toward_zero = couple(blocks(upper_top, 0), pattern(3, 0), down_top)
    final_two = solve(toward_two, fore_two, upper_list[2], False)
    down_two = copy_out(final_two)
    toward_one = toward_one + couple(blocks(upper_sub, 2), pattern(2, 2), down_two)
    toward_zero = toward_zero + couple(blocks(upper_sub, 1), pattern(2, 1), down_two)
    final_one = solve(toward_one, fore_one, upper_list[1], False)
    down_one = copy_out(final_one)
    toward_zero = toward_zero + couple(blocks(upper_sub, 0), pattern(2, 0), down_one)
    final_zero = solve(toward_zero, fore_zero, upper_list[0], False)
    solution_sub = jnp.stack([keep_rows(final_zero), keep_rows(final_one), keep_rows(final_two)])[
        None, :, :, None
    ]
    solution_top = keep_rows(final_top)[:, None]
    return (solution_sub, solution_top)


def solution(mesh):
    placed = (
        P("layer", None, None, "row", "col", None),
        P(None, "row", "col", None),
        P("layer", None, None, "row", "col", None),
        P(None, "row", "col", None),
        P("layer", None, None, "row", "col", None),
        P(None, "row", "col", None),
        P("layer", None, None, "row", None, "col", None, None),
        P("layer", None, None, "row", None, "col", None, None),
        P("layer", None, None, "row", None, "col", None, None),
        P("layer", None, None, "row", None, "col", None, None),
        P("layer", None, None, None, "row", None, "col"),
    )
    layers, grid = mesh.shape["layer"], mesh.shape["row"]

    def choose(*arguments):
        rhs_sub, rhs_top, inverse = arguments[0], arguments[1], arguments[3]
        columns, width = rhs_top.shape[-1] // grid, inverse.shape[-1]
        square = mesh.shape["row"] == mesh.shape["col"] and rhs_sub.shape[2] == 1
        held = 4 * 4 * LEVELS * grid * width * width
        if square and grid == 4 and rhs_top.shape[-1] % (128 * grid) == 0 and held <= 2**24:
            return solve_in_kernel(layers, grid, *arguments)
        return on_device(*arguments)

    return jax.shard_map(
        choose,
        mesh=mesh,
        in_specs=placed,
        out_specs=(P("layer", None, None, "row", "col", None), P(None, "row", "col", None)),
        check_vma=False,
    )
```
